32 devices in a mesh: grp: 2 (over x), scen: 16 (over z, y, core).
Axes of the slice: x: 2, y: 2, z: 4, core: 2. Of those that a mesh axis runs over, the one named last changes fastest.
Arguments:
- returns: bfloat16 [64, 32768], P(None, ('grp', 'scen')), parts along dimension 1, may hold values from -2 to 2
- exposures: bfloat16 [32768, 64], P(('grp', 'scen')), parts along dimension 0, may hold values from -0.75 to 0.75
- guarantees: float32 [32768], P(('grp', 'scen')), parts along dimension 0, may hold values from 0.7 to 1.3
- guar_type: int32 [32768], P(('grp', 'scen')), parts along dimension 0, may hold values from 0 to 2
- line_ids: int32 [32768], P(('grp', 'scen')), parts along dimension 0, may hold values from 0 to 63
- drivers: float32 [40, 32768], P(None, ('grp', 'scen')), parts along dimension 1, may hold values from -1.7 to 1.7
- exponents: int32 [512, 40], replicated, may hold values from 0 to 3, as said below
Outputs:
- gram: float32 [1024, 512], P('grp'), parts along dimension 0
- rhs: float32 [1024, 64], P('grp'), parts along dimension 0
The draws below stay inside these ranges and needn't reach their ends.
There are 2 independent parts, one for each index of `grp`. The reference program is written for one: setup_inputs(seed, part) draws one part's arguments, and reference() takes and returns one part's arrays. A program takes and returns all parts, laid end to end along the dimension named above; an argument that names none is the same for every part. Nothing has to cross between parts.
Inputs may be any that keep to these rules, and one draw needn't show every extreme that they name: Each row of exponents sums to 3, and every eighth row (0, 8, 16, ...) is one driver cubed.
All inputs are finite; a program needn't handle non-finite values.
Results may differ from the reference program's by a relative error of at most 0.009.
Values may be sent and summed in bfloat16 or wider, within the bound.
No kernel may reach another device: no remote copies, remote signals or barrier semaphores. Data moves between devices by JAX's collectives and lax.ppermute only.
A program may use at most 320 MiB of HBM per device.

```python
import math
import jax
import jax.numpy as jnp
from jax import lax

FACTORS = 64
LINES = 64
TERMS = 512
DRIVERS = 40
MP_DEV = 1024
SCEN = 16384
POINTS = 16384


def draw_exponents(key, part):
    first_key, second_key, third_key = jax.random.split(jax.random.fold_in(key, 17), 3)
    first = jax.random.randint(first_key, (TERMS,), 0, DRIVERS)
    second = jax.random.randint(second_key, (TERMS,), 0, DRIVERS)
    third = jax.random.randint(third_key, (TERMS,), 0, DRIVERS)
    rows = jnp.arange(TERMS)
    cubed = rows % 8 == 0
    second = jnp.where(cubed, first, second)
    third = jnp.where(cubed, first, third)
    cols = jnp.arange(DRIVERS)[None, :]
    counts = (first[:, None] == cols).astype(jnp.int32) + (second[:, None] == cols).astype(jnp.int32) + (third[:, None] == cols).astype(jnp.int32)
    return counts.astype(jnp.int32)


def set_ends(values, rng, low, high):
    shape = values.shape
    index_at = [jax.random.randint(jax.random.fold_in(rng, axis), (), 0, shape[axis]) for axis in range(len(shape))]
    values = values.at[tuple(index_at)].set(low)
    longest = shape.index(max(shape))
    index_at[longest] = (index_at[longest] + 1) % shape[longest]
    return values.at[tuple(index_at)].set(high)


def steps_of(key, shape, cuts, low, high):
    gain, own = 1.0, jax.random.fold_in(key, 6)
    for axis_at, blocks in cuts:
        heights = jnp.exp(jax.random.uniform(jax.random.fold_in(own, axis_at), (blocks,), jnp.float32, low / len(cuts), high / len(cuts)))
        gain = gain * jnp.repeat(heights, shape[axis_at] // blocks).reshape([-1 if axis == axis_at else 1 for axis in range(len(shape))])
    return gain


def bell_draw(own_key, shape, width, limit, cuts=(), kind=jnp.bfloat16):
    gain = steps_of(own_key, shape, cuts, -0.22, 0.18) if cuts else 1.0
    result = jax.random.normal(own_key, shape, jnp.float32) * width * gain
    return jnp.minimum(jnp.maximum(result, -limit), limit).astype(kind)


def setup_inputs(seed: int = 0, part: int = 0) -> dict:
    seeds = jax.random.split(jax.random.key(seed), 8)
    own_keys = jax.random.split(jax.random.fold_in(seeds[7], part), 8)
    return {
        "returns": bell_draw(own_keys[0], (FACTORS, SCEN), 0.3, 2.0, ((1, 16),)),
        "exposures": bell_draw(own_keys[1], (POINTS, FACTORS), FACTORS ** -0.5, 0.75, ((0, 16),)),
        "guarantees": jnp.clip(0.7 + 0.59999996 * jax.random.uniform(own_keys[2], (POINTS,), jnp.float32) ** steps_of(own_keys[2], (POINTS,), ((0, 16),), -0.2, 0.2), 0.7, 1.3),
        "guar_type": set_ends(jax.random.randint(own_keys[3], (POINTS,), 0, 3), jax.random.fold_in(own_keys[3], 1), 0, 2).astype(jnp.int32),
        "line_ids": set_ends(jax.random.randint(own_keys[4], (POINTS,), 0, LINES), jax.random.fold_in(own_keys[4], 1), 0, LINES - 1).astype(jnp.int32),
        "drivers": jnp.clip(jax.random.uniform(own_keys[5], (DRIVERS, SCEN), jnp.float32, -1.7, 1.7) * steps_of(own_keys[5], (DRIVERS, SCEN), ((1, 16),), -0.4, 0.0), -1.7, 1.7),
        "exponents": draw_exponents(jax.random.fold_in(seeds[7], 71), part),
    }


def basis_of(drivers, exponents):
    basis = jnp.ones((exponents.shape[0], drivers.shape[1]), jnp.float32)
    for j in range(drivers.shape[0]):
        power = exponents[:, j][:, None]
        value = drivers[j][None, :]
        factor = jnp.where(power == 1, value, jnp.where(power == 2, value * value, jnp.where(power == 3, value * value * value, jnp.float32(1.0))))
        basis = basis * factor
    return basis

def reference(returns, exposures, guarantees, guar_type, line_ids, drivers, exponents):
    blocks = POINTS // MP_DEV
    exp_blocks = exposures.reshape(blocks, MP_DEV, FACTORS)
    guar_blocks = guarantees.reshape(blocks, MP_DEV)
    type_blocks = guar_type.reshape(blocks, MP_DEV)
    line_blocks = line_ids.reshape(blocks, MP_DEV)
    labels = jnp.arange(LINES, dtype=jnp.int32)[:, None]

    def step(total, items):
        exp_rows, guar_rows, type_rows, line_rows = items
        fund = jnp.exp(jnp.dot(exp_rows, returns, preferred_element_type=jnp.float32))
        level = guar_rows * (1.0 + 0.15 * type_rows.astype(jnp.float32))
        payoff = jnp.maximum(level[:, None] - fund, 0.0)
        onehot = (line_rows[None, :] == labels).astype(jnp.float32)
        return (total + jnp.dot(onehot, payoff, precision=lax.Precision.HIGHEST), None)
    total, _ = lax.scan(step, jnp.zeros((LINES, SCEN), jnp.float32), (exp_blocks, guar_blocks, type_blocks, line_blocks))
    line_value = total / math.sqrt(POINTS / LINES)
    basis = basis_of(drivers, exponents)
    gram = jnp.dot(basis, basis.T, precision=lax.Precision.HIGHEST) / SCEN
    rhs = jnp.dot(basis, line_value.T, precision=lax.Precision.HIGHEST) / SCEN
    return (gram, rhs)
```

```python
import functools
import math

import jax
import jax.numpy as jnp
from jax import lax
from jax.experimental import pallas as pl
from jax.experimental.pallas import tpu as pltpu
from jax.sharding import PartitionSpec as P

LINES = 64
TAIL = 16
CHUNK = 512
LOG2E = 1.4426950408889634
BF = jnp.bfloat16
F32 = jnp.float32
VMEM = 56 * 2**20


def params():
    return pltpu.CompilerParams(vmem_limit_bytes=VMEM)


def three_parts(x):
    a = x.astype(BF)
    b = (x - a.astype(F32)).astype(BF)
    c = (x - a.astype(F32) - b.astype(F32)).astype(BF)
    return a, b, c


def value_kernel(factors, count, *refs):
    rets, packs, out, rt, w, oh, lev = refs[0:2], refs[2 : 2 + count], *refs[2 + count :]
    own = rets[0].shape[1]
    for i in range(2):
        r = rets[i][...].astype(F32).T.astype(BF)
        rt[i * own : (i + 1) * own, :factors] = r
        rt[i * own : (i + 1) * own, factors:] = r
    points = packs[0].shape[1]
    lines = oh.shape[0]
    for i in range(count):
        at = slice(i * points, (i + 1) * points)
        e = packs[i][:factors, :].astype(F32) * LOG2E
        high = e.astype(BF)
        w[:factors, at] = high
        w[factors:, at] = (e - high.astype(F32)).astype(BF)
        tail = packs[i][factors:, :].astype(F32)
        lev[:, at] = tail[0:1] + tail[1:2] + tail[2:3]
        label = lax.broadcasted_iota(jnp.int32, (lines, points), 0).astype(F32)
        oh[:, at] = (label == tail[3:4]).astype(BF)

    def step(i, carry):
        s0 = pl.multiple_of(i * CHUNK, CHUNK)
        r = rt[pl.ds(s0, CHUNK), :]
        total = None
        for j in range(count):
            at = slice(j * points, (j + 1) * points)
            power = jnp.dot(r, w[:, at], preferred_element_type=F32)
            payoff = jnp.maximum(lev[:, at] - jnp.exp2(power), 0.0).astype(BF)
            part = lax.dot_general(
                payoff, oh[:, at], (((1,), (1,)), ((), ())), preferred_element_type=F32
            )
            total = part if total is None else total + part
        out[pl.ds(s0, CHUNK), :] = total
        return carry

    lax.fori_loop(0, 2 * own // CHUNK, step, 0)


def values_of(rets, packs, lines):
    factors, own = rets[0].shape
    points = packs[0].shape[1]
    count = len(packs)
    pairs = 2 * own * points * count
    return pl.pallas_call(
        functools.partial(value_kernel, factors, count),
        out_shape=jax.ShapeDtypeStruct((2 * own, lines), F32),
        scratch_shapes=[
            pltpu.VMEM((2 * own, 2 * factors), BF),
            pltpu.VMEM((2 * factors, points * count), BF),
            pltpu.VMEM((lines, points * count), BF),
            pltpu.VMEM((1, points * count), F32),
        ],
        compiler_params=params(),
        cost_estimate=pl.CostEstimate(
            flops=1700 * pairs, bytes_accessed=2**20, transcendentals=pairs
        ),
    )(*rets, *packs)


def basis_kernel(half, exps, d0, d1, high, low, gram):
    terms, count = exps.shape
    own = d0.shape[1]
    e = exps[...].astype(F32)
    row = lax.broadcasted_iota(jnp.int32, (count, count), 0)
    col = lax.broadcasted_iota(jnp.int32, (count, count), 1)
    upto = (row <= col).astype(BF)
    cum = jnp.dot(e.astype(BF), upto, preferred_element_type=F32)
    before = cum - e
    picks = [
        jnp.where((cum > t + 0.5) & (before < t + 0.5), 1.0, 0.0).astype(BF) for t in range(3)
    ]
    picks = [jnp.concatenate([p, p, p], axis=1) for p in picks]
    for i, d in enumerate((d0, d1)):
        parts = jnp.concatenate(three_parts(d[...]), axis=0)
        for c in range(own // CHUNK):
            part = parts[:, c * CHUNK : (c + 1) * CHUNK]
            x = [jnp.dot(p, part, preferred_element_type=F32) for p in picks]
            b = x[0] * x[1] * x[2]
            h = b.astype(BF)
            at = slice(i * own + c * CHUNK, i * own + (c + 1) * CHUNK)
            high[:, at] = h
            low[:, at] = (b - h.astype(F32)).astype(BF)
    rows = terms // 2
    r0 = pl.multiple_of(half[0] * rows, rows)
    gram[...] = lax.dot_general(
        high[pl.ds(r0, rows), :], high[...], (((1,), (1,)), ((), ())), preferred_element_type=F32
    )


def basis_of(half, exponents, drivers):
    terms, _ = exponents.shape
    own = drivers[0].shape[1]
    return pl.pallas_call(
        basis_kernel,
        in_specs=[pl.BlockSpec(memory_space=pltpu.SMEM)]
        + [pl.BlockSpec(memory_space=pltpu.VMEM)] * 3,
        out_shape=(
            jax.ShapeDtypeStruct((terms, 2 * own), BF),
            jax.ShapeDtypeStruct((terms, 2 * own), BF),
            jax.ShapeDtypeStruct((terms // 2, terms), F32),
        ),
        compiler_params=params(),
        cost_estimate=pl.CostEstimate(
            flops=6 * 10**9, bytes_accessed=6 * 2**20, transcendentals=0
        ),
    )(half, exponents, *drivers)


def rhs_kernel(scale, count, high, low, *refs):
    values, out = refs[:count], refs[count]
    v = values[0][...]
    for other in values[1:]:
        v = v + other[...]
    lines = v.shape[1]
    vh = v.astype(BF)
    vl = (v - vh.astype(F32)).astype(BF)
    both = jnp.concatenate([vh, vl], axis=1)
    a = jnp.dot(high[...], both, preferred_element_type=F32)
    b = jnp.dot(low[...], vh, preferred_element_type=F32)
    out[...] = ((a[:, :lines] + a[:, lines:] + b) * scale).T


def rhs_of(scale, high, low, values):
    terms = high.shape[0]
    lines = values[0].shape[1]
    return pl.pallas_call(
        functools.partial(rhs_kernel, scale, len(values)),
        out_shape=jax.ShapeDtypeStruct((lines, terms), F32),
        compiler_params=params(),
        cost_estimate=pl.CostEstimate(
            flops=3 * 10**9, bytes_accessed=6 * 2**20, transcendentals=0
        ),
    )(high, low, *values)


def place_kernel(scale, blocks, *refs):
    order, pieces, out = refs[0], refs[1:-1], refs[-1]
    rows = out.shape[0] // blocks
    k = 0
    for piece in pieces:
        for i in range(piece.shape[0] // rows):
            at = pl.multiple_of(order[k] * rows, rows)
            out[pl.ds(at, rows), :] = piece[i * rows : (i + 1) * rows, :] * scale
            k += 1


def placed(scale, blocks, order, pieces, terms):
    return pl.pallas_call(
        functools.partial(place_kernel, scale, blocks),
        in_specs=[pl.BlockSpec(memory_space=pltpu.SMEM)]
        + [pl.BlockSpec(memory_space=pltpu.VMEM)] * len(pieces),
        out_shape=jax.ShapeDtypeStruct((terms, terms), F32),
        compiler_params=params(),
        cost_estimate=pl.CostEstimate(
            flops=2**20, bytes_accessed=2 * 2**20, transcendentals=0
        ),
    )(order, *pieces)


def local(n, returns, exposures, guarantees, guar_type, line_ids, drivers, exponents):
    lines = LINES
    scen_total = returns.shape[1] * n
    all_points = exposures.shape[0] * n
    terms = exponents.shape[0]
    me = lax.axis_index("scen")

    def swap(x, mask):
        return lax.ppermute(x, "scen", [(i, i ^ mask) for i in range(n)])

    def bit(mask):
        return (me // mask) % 2

    far = [m for m in range(4, n, 4)]
    level = guarantees * (1.0 + 0.15 * guar_type.astype(F32))
    rows = [*three_parts(level), line_ids.astype(BF)]
    rows = jnp.stack(rows + [jnp.zeros_like(rows[0])] * (TAIL - 4))
    pack = jnp.concatenate([exposures.T, rows], axis=0)

    rets = (returns, swap(returns, 2))
    packs = {0: pack, 1: swap(pack, 1)}
    for m in far:
        packs[m] = swap(pack, m)
        packs[m ^ 1] = swap(packs[m], 1)
    both = (drivers, swap(drivers, 2))

    half = bit(2).astype(jnp.int32).reshape(1)
    high, low, gram = basis_of(half, exponents, both)

    groups = [[0, 1], [4, 5]] + [[m, m ^ 1, m + 4, m ^ 5] for m in range(8, n, 8)]
    values = [values_of(rets, [packs[k] for k in g], lines) for g in groups]
    scale = 1.0 / (math.sqrt(all_points / lines) * scen_total)
    rhs = rhs_of(scale, high, low, values)

    masks = [1] + [4 << i for i in range((n // 4).bit_length() - 1)]
    for m in masks:
        size = gram.shape[0] // 2
        mine = lax.dynamic_slice_in_dim(gram, bit(m) * size, size, 0)
        theirs = lax.dynamic_slice_in_dim(gram, (1 - bit(m)) * size, size, 0)
        gram = mine + swap(theirs, m)
    pieces, order = [gram], [0]
    for m in [*masks[:0:-1], 2, 1]:
        sent = pieces[0] if len(pieces) == 1 else jnp.concatenate(pieces, axis=0)
        pieces.append(swap(sent, m))
        order += [k ^ m for k in order]

    def block_of(k):
        who = me ^ k
        place = (who // 2) % 2
        for m in masks:
            place = place * 2 + (who // m) % 2
        return place

    order = jnp.stack([block_of(k) for k in order]).astype(jnp.int32)
    gram = placed(1.0 / scen_total, n, order, pieces, terms)

    for m in [1, 2] + masks[1:]:
        rhs = rhs + swap(rhs, m)
    return (gram, rhs.T)


def solution(mesh):
    spots = (
        P(None, ("grp", "scen")),
        P(("grp", "scen"), None),
        P(("grp", "scen")),
        P(("grp", "scen")),
        P(("grp", "scen")),
        P(None, ("grp", "scen")),
        P(),
    )
    return jax.shard_map(
        functools.partial(local, mesh.shape["scen"]),
        mesh=mesh,
        in_specs=spots,
        out_specs=(P("grp", None), P("grp", None)),
        check_vma=False,
    )
```

```python
import functools
import math

import jax
import jax.numpy as jnp
from jax import lax
from jax.experimental import pallas as pl
from jax.experimental.pallas import tpu as pltpu
from jax.sharding import PartitionSpec as P

LINES = 64
TAIL = 16
CHUNK = 512
LOG2E = 1.4426950408889634
BF = jnp.bfloat16
F32 = jnp.float32
VMEM = 24 * 2**20


def params():
    return pltpu.CompilerParams(vmem_limit_bytes=VMEM)


def three_parts(x):
    a = x.astype(BF)
    b = (x - a.astype(F32)).astype(BF)
    c = (x - a.astype(F32) - b.astype(F32)).astype(BF)
    return a, b, c


def value_kernel(plan, count, earlier, scale, *refs):
    blocks = len(plan)
    rts, refs = refs[:blocks], refs[blocks:]
    packs, refs = refs[:count], refs[count:]
    if scale:
        before, refs = refs[: len(earlier)], refs[len(earlier) :]
        basis, refs = refs[: 2 * blocks], refs[2 * blocks :]
        out, w, oh, lev, held, sems = refs
        loads = [
            pltpu.make_async_copy(basis[i], held.at[i], sems.at[i]) for i in range(2 * blocks)
        ]
        for load in loads:
            load.start()
    else:
        outs, (w, oh, lev) = refs[:blocks], refs[blocks:]
    own, double = rts[0].shape
    factors = double // 2
    points = packs[0].shape[1]
    lines = oh.shape[0]
    for i in range(count):
        at = slice(i * points, (i + 1) * points)
        e = packs[i][:factors, :].astype(F32) * LOG2E
        high = e.astype(BF)
        w[:factors, at] = high
        w[factors:, at] = (e - high.astype(F32)).astype(BF)
        tail = packs[i][factors:, :].astype(F32)
        lev[:, at] = tail[0:1] + tail[1:2] + tail[2:3]
        label = lax.broadcasted_iota(jnp.int32, (lines, points), 0).astype(F32)
        oh[:, at] = (label == tail[3:4]).astype(BF)
    sums = []
    for i in range(blocks):
        for s0 in range(0, own, CHUNK):
            r = rts[i][s0 : s0 + CHUNK, :]
            total = None
            for j in plan[i]:
                at = slice(j * points, (j + 1) * points)
                power = jnp.dot(r, w[:, at], preferred_element_type=F32)
                payoff = jnp.maximum(lev[:, at] - jnp.exp2(power), 0.0).astype(BF)
                part = lax.dot_general(
                    payoff, oh[:, at], (((1,), (1,)), ((), ())), preferred_element_type=F32
                )
                total = part if total is None else total + part
            if not scale:
                outs[i][s0 : s0 + CHUNK, :] = total
                continue
            for k, at in enumerate(earlier):
                if at == i:
                    total = total + before[k][s0 : s0 + CHUNK, :]
            sums.append((i, s0, total))
    if not scale:
        return
    for load in loads:
        load.wait()
    result = None
    for i in range(blocks):
        v = jnp.concatenate([t for at, _, t in sums if at == i], axis=0)
        vh = v.astype(BF)
        vl = (v - vh.astype(F32)).astype(BF)
        both = jnp.concatenate([vh, vl], axis=1)
        a = jnp.dot(held[2 * i], both, preferred_element_type=F32)
        b = jnp.dot(held[2 * i + 1], vh, preferred_element_type=F32)
        part = a[:, :lines] + a[:, lines:] + b
        result = part if result is None else result + part
    out[...] = (result * scale).T


def values_of(rts, packs, plan, lines, before=(), basis=(), scale=None):
    own, double = rts[0].shape
    points = packs[0].shape[1]
    count = len(packs)
    pairs = own * points * sum(len(p) for p in plan)
    scratch = [
        pltpu.VMEM((double, points * count), BF),
        pltpu.VMEM((lines, points * count), BF),
        pltpu.VMEM((1, points * count), F32),
    ]
    specs = [pl.BlockSpec(memory_space=pltpu.VMEM)] * (len(rts) + count + len(before))
    if scale:
        terms = basis[0].shape[0]
        specs += [pl.BlockSpec(memory_space=pl.ANY)] * len(basis)
        scratch += [
            pltpu.VMEM((len(basis), terms, own), BF),
            pltpu.SemaphoreType.DMA((len(basis),)),
        ]
        shape = jax.ShapeDtypeStruct((lines, terms), F32)
    else:
        shape = [jax.ShapeDtypeStruct((own, lines), F32)] * len(rts)
    kernel = functools.partial(value_kernel, plan, count, [i for i, _ in before], scale)
    return pl.pallas_call(
        kernel,
        in_specs=specs,
        out_shape=shape,
        scratch_shapes=scratch,
        compiler_params=params(),
        cost_estimate=pl.CostEstimate(
            flops=1700 * pairs, bytes_accessed=2**20, transcendentals=pairs
        ),
    )(*rts, *packs, *[v for _, v in before], *basis)


def picks_of(exps):
    count = exps.shape[1]
    e = exps[...].astype(F32)
    row = lax.broadcasted_iota(jnp.int32, (count, count), 0)
    col = lax.broadcasted_iota(jnp.int32, (count, count), 1)
    upto = (row <= col).astype(BF)
    cum = jnp.dot(e.astype(BF), upto, preferred_element_type=F32)
    before = cum - e
    picks = [
        jnp.where((cum > t + 0.5) & (before < t + 0.5), 1.0, 0.0).astype(BF) for t in range(3)
    ]
    return [jnp.concatenate([p, p, p], axis=1) for p in picks]


def basis_kernel(exps, drivers, returns, high, low, rt):
    factors = returns.shape[0]
    r = returns[...].astype(F32).T.astype(BF)
    rt[:, :factors] = r
    rt[:, factors:] = r
    picks = picks_of(exps)
    parts = jnp.concatenate(three_parts(drivers[...]), axis=0)
    for c in range(0, drivers.shape[1], CHUNK):
        x = [jnp.dot(p, parts[:, c : c + CHUNK], preferred_element_type=F32) for p in picks]
        b = x[0] * x[1] * x[2]
        h = b.astype(BF)
        high[:, c : c + CHUNK] = h
        low[:, c : c + CHUNK] = (b - h.astype(F32)).astype(BF)


def gram_kernel(start, exps, drivers, returns, first, high, low, rt, keep, send):
    basis_kernel(exps, drivers, returns, high, low, rt)
    rows = keep.shape[0]
    for i, out in enumerate((keep, send)):
        r0 = pl.multiple_of(start[i] * rows, rows)
        out[...] = lax.dot_general(
            first[pl.ds(r0, rows), :],
            first[...],
            (((1,), (1,)), ((), ())),
            preferred_element_type=F32,
        ) + lax.dot_general(
            high[pl.ds(r0, rows), :],
            high[...],
            (((1,), (1,)), ((), ())),
            preferred_element_type=F32,
        )


def basis_of(exponents, drivers, returns, start=None, first=None):
    terms = exponents.shape[0]
    factors, own = returns.shape
    shapes = [jax.ShapeDtypeStruct((terms, own), BF)] * 2
    shapes.append(jax.ShapeDtypeStruct((own, 2 * factors), BF))
    vmem = pl.BlockSpec(memory_space=pltpu.VMEM)
    cost = pl.CostEstimate(flops=3 * 10**9, bytes_accessed=3 * 2**20, transcendentals=0)
    if start is None:
        return pl.pallas_call(
            basis_kernel, out_shape=shapes, compiler_params=params(), cost_estimate=cost
        )(exponents, drivers, returns)
    shapes += [jax.ShapeDtypeStruct((terms // 4, terms), F32)] * 2
    return pl.pallas_call(
        gram_kernel,
        in_specs=[pl.BlockSpec(memory_space=pltpu.SMEM)] + [vmem] * 4,
        out_shape=shapes,
        compiler_params=params(),
        cost_estimate=cost,
    )(start, exponents, drivers, returns, first)


def split_kernel(order, keep, more, *outs):
    rows = outs[0].shape[0]
    for i, out in enumerate(outs):
        at = pl.ds(pl.multiple_of(order[i] * rows, rows), rows)
        out[...] = keep[at, :] + more[at, :]


def split(order, keep, more, count):
    rows, terms = keep.shape
    return pl.pallas_call(
        split_kernel,
        in_specs=[pl.BlockSpec(memory_space=pltpu.SMEM)]
        + [pl.BlockSpec(memory_space=pltpu.VMEM)] * 2,
        out_shape=[jax.ShapeDtypeStruct((rows // count, terms), F32)] * count,
        compiler_params=params(),
        cost_estimate=pl.CostEstimate(flops=2**20, bytes_accessed=2**19, transcendentals=0),
    )(order, keep, more)


def place_kernel(scale, blocks, *refs):
    order, pieces, out = refs[0], refs[1:-1], refs[-1]
    rows = out.shape[0] // blocks
    k = 0
    for piece in pieces:
        for i in range(piece.shape[0] // rows):
            at = pl.multiple_of(order[k] * rows, rows)
            out[pl.ds(at, rows), :] = piece[i * rows : (i + 1) * rows, :] * scale
            k += 1


def placed(scale, blocks, order, pieces, terms):
    return pl.pallas_call(
        functools.partial(place_kernel, scale, blocks),
        in_specs=[pl.BlockSpec(memory_space=pltpu.SMEM)]
        + [pl.BlockSpec(memory_space=pltpu.VMEM)] * len(pieces),
        out_shape=jax.ShapeDtypeStruct((terms, terms), F32),
        compiler_params=params(),
        cost_estimate=pl.CostEstimate(
            flops=2**20, bytes_accessed=2 * 2**20, transcendentals=0
        ),
    )(order, *pieces)


def after(x, done):
    return lax.optimization_barrier((x, done))[0]


def local(n, returns, exposures, guarantees, guar_type, line_ids, drivers, exponents):
    lines = LINES
    scen_total = returns.shape[1] * n
    all_points = exposures.shape[0] * n
    terms = exponents.shape[0]
    me = lax.axis_index("scen").astype(jnp.int32)
    core, side, depth = me & 1, (me >> 1) & 1, me >> 2

    def swap(x, mask):
        return lax.ppermute(x, "scen", [(i, i ^ mask) for i in range(n)])

    far = list(range(4, n, 4))
    level = guarantees * (1.0 + 0.15 * guar_type.astype(F32))
    rows = [*three_parts(level), line_ids.astype(BF)]
    rows = jnp.stack(rows + [jnp.zeros_like(rows[0])] * (TAIL - 4))
    pack = jnp.concatenate([exposures.T, rows], axis=0)

    packs = {0: pack, 1: swap(pack, 1)}
    returns1 = swap(returns, 2)
    for m in far:
        packs[m] = swap(pack, m)
        packs[m ^ 1] = swap(packs[m], 1)
    drivers1 = swap(after(drivers, pack), 2)

    high0, low0, rt0 = basis_of(exponents, after(drivers, pack), returns)
    (v,) = values_of([after(rt0, low0)], [packs[0], packs[1]], [[0, 1]], lines)
    before = [(0, v)]

    base = side * 2 + core
    start = jnp.stack([base, base ^ 1])
    high1, low1, rt1, keep, send = basis_of(
        exponents, after(drivers1, v), returns1, start, high0
    )
    more = swap(send, 1)
    (v,) = values_of([rt1], [packs[0], packs[1]], [[0, 1]], lines)
    before.append((1, v))

    near = jnp.stack([depth ^ (m // 4) for m in [0] + far])
    keep, more = after((keep, more), v)
    parts = split(near, keep, more, n // 4)
    share = parts[0]
    for m, part in zip(far, parts[1:], strict=True):
        share = share + swap(part, m)

    scale = 1.0 / (math.sqrt(all_points / lines) * scen_total)
    tie = parts[0]
    for m in far[:-1]:
        duo = after((packs[m], packs[m ^ 1]), tie)
        v0, v1 = values_of([rt0, rt1], duo, [[0, 1], [0, 1]], lines)
        before += [(0, v0), (1, v1)]
        tie = v0
    tie = share = after(share, tie)
    duo = after((packs[far[-1]], packs[far[-1] ^ 1]), tie)
    basis = (high0, low0, high1, low1)
    rhs = values_of([rt0, rt1], duo, [[0, 1], [0, 1]], lines, before, basis, scale)

    a = jnp.concatenate([share] + [swap(share, m) for m in far], axis=0)
    b = swap(a, 2)
    c, d = swap(a, 1), swap(b, 1)
    order = jnp.concatenate([near + (base ^ k) * (n // 4) for k in (0, 2, 1, 3)])
    gram = placed(1.0 / scen_total, n, order, [a, b, c, d], terms)

    for m in [1, 2] + [4 << i for i in range((n // 4).bit_length() - 1)]:
        rhs = rhs + swap(rhs, m)
    return (gram, rhs.T)


def solution(mesh):
    spots = (
        P(None, ("grp", "scen")),
        P(("grp", "scen"), None),
        P(("grp", "scen")),
        P(("grp", "scen")),
        P(("grp", "scen")),
        P(None, ("grp", "scen")),
        P(),
    )
    return jax.shard_map(
        functools.partial(local, mesh.shape["scen"]),
        mesh=mesh,
        in_specs=spots,
        out_specs=(P("grp", None), P("grp", None)),
        check_vma=False,
    )
```

```python
import functools
import math

import jax
import jax.numpy as jnp
from jax import lax
from jax.experimental import pallas as pl
from jax.experimental.pallas import tpu as pltpu
from jax.sharding import PartitionSpec as P

LINES = 64
TAIL = 16
CHUNK = 512
LOG2E = 1.4426950408889634
BF = jnp.bfloat16
F32 = jnp.float32
HALF = jnp.float16
VMEM = 24 * 2**20


def params(limit=VMEM):
    return pltpu.CompilerParams(vmem_limit_bytes=limit)


def parts_of(x, count):
    parts = []
    for _ in range(count):
        parts.append(x.astype(BF).astype(F32))
        x = x - parts[-1]
    return parts


def pack_kernel(*refs):
    points, scens = refs[6:8]
    held, sems = refs[8:14], refs[14]
    loads = [pltpu.make_async_copy(refs[i], held[i], sems.at[i]) for i in range(6)]
    for load in loads:
        load.start()
    for load in loads:
        load.wait()
    exposures, guarantees, kinds, lines, returns, drivers = held
    factors = exposures.shape[0]
    points[:factors, :] = exposures[...]
    level = guarantees[...] * (1.0 + 0.15 * kinds[...].astype(F32))
    rows = [*parts_of(level, 3), lines[...].astype(F32)]
    rows.append(jnp.zeros((TAIL - 4, level.shape[1]), F32))
    points[factors:, :] = jnp.concatenate(rows, axis=0).astype(BF)
    scens[:factors, :] = returns[...]
    scens[factors:, :] = jnp.concatenate(parts_of(drivers[...], 2), axis=0).astype(BF)


def packs_of(exposures, guarantees, kinds, lines, returns, drivers):
    points, factors = exposures.shape
    row = (1, points)
    args = (
        exposures.T,
        guarantees.reshape(row),
        kinds.reshape(row),
        lines.reshape(row),
        returns,
        drivers,
    )
    return pl.pallas_call(
        pack_kernel,
        in_specs=[pl.BlockSpec(memory_space=pltpu.HBM)] * len(args),
        out_shape=[
            jax.ShapeDtypeStruct((factors + TAIL, points), BF),
            jax.ShapeDtypeStruct((factors + 2 * drivers.shape[0], returns.shape[1]), BF),
        ],
        scratch_shapes=[pltpu.VMEM(a.shape, a.dtype) for a in args]
        + [pltpu.SemaphoreType.DMA((len(args),))],
        compiler_params=params(58 * 2**20),
        cost_estimate=pl.CostEstimate(flops=2**20, bytes_accessed=2**20, transcendentals=0),
    )(*args)


def value_kernel(plan, count, earlier, scale, *refs):
    blocks = len(plan)
    rts, refs = refs[:blocks], refs[blocks:]
    stacks, refs = refs[:count], refs[count:]
    if scale:
        before, refs = refs[: len(earlier)], refs[len(earlier) :]
        basis, refs = refs[: 2 * blocks], refs[2 * blocks :]
        core, keep, send, w, oh, lev, whole = refs
    else:
        outs, (w, oh, lev) = refs[:blocks], refs[blocks:]
    own, double = rts[0].shape
    factors = double // 2
    points = stacks[0].shape[1]
    lines = oh.shape[0]
    height = factors + TAIL
    packs = [s.at[k : k + height] for s in stacks for k in range(0, s.shape[0], height)]
    for i in range(len(packs)):
        at = slice(i * points, (i + 1) * points)
        e = packs[i][:factors, :].astype(F32) * LOG2E
        high = e.astype(BF)
        w[:factors, at] = high
        w[factors:, at] = (e - high.astype(F32)).astype(BF)
        tail = packs[i][factors:, :].astype(F32)
        lev[:, at] = tail[0:1] + tail[1:2] + tail[2:3]
        label = lax.broadcasted_iota(jnp.int32, (lines, points), 0).astype(F32)
        oh[:, at] = (label == tail[3:4]).astype(BF)
    sums = []
    for i in range(blocks):
        for s0 in range(0, own, CHUNK):
            r = rts[i][s0 : s0 + CHUNK, :]
            total = None
            for j in plan[i] or range(len(packs)):
                at = slice(j * points, (j + 1) * points)
                power = jnp.dot(r, w[:, at], preferred_element_type=F32)
                payoff = jnp.maximum(lev[:, at] - jnp.exp2(power), 0.0).astype(BF)
                part = lax.dot_general(
                    payoff, oh[:, at], (((1,), (1,)), ((), ())), preferred_element_type=F32
                )
                total = part if total is None else total + part
            if not scale:
                outs[i][s0 : s0 + CHUNK, :] = total
                continue
            for k, at in enumerate(earlier):
                if at == i:
                    total = total + before[k][s0 : s0 + CHUNK, :]
            sums.append((i, s0, total))
    if not scale:
        return
    result = None
    for i in range(blocks):
        v = jnp.concatenate([t for at, _, t in sums if at == i], axis=0)
        vh = v.astype(BF)
        vl = (v - vh.astype(F32)).astype(BF)
        both = jnp.concatenate([vh, vl], axis=1)
        a = jnp.dot(basis[2 * i][...], both, preferred_element_type=F32)
        b = jnp.dot(basis[2 * i + 1][...], vh, preferred_element_type=F32)
        part = a[:, :lines] + a[:, lines:] + b
        result = part if result is None else result + part
    whole[...] = (result * scale).T
    half = lines // 2
    keep[...] = whole[pl.ds(pl.multiple_of(core[0] * half, half), half), :]
    send[...] = whole[pl.ds(pl.multiple_of((1 - core[0]) * half, half), half), :]


def values_of(rts, packs, plan, lines, before=(), basis=(), scale=None, core=None):
    own, double = rts[0].shape
    points = packs[0].shape[1]
    count = sum(p.shape[0] for p in packs) // (double // 2 + TAIL)
    pairs = own * points * len(plan) * count
    scratch = [
        pltpu.VMEM((double, points * count), BF),
        pltpu.VMEM((lines, points * count), BF),
        pltpu.VMEM((1, points * count), F32),
    ]
    specs = [pl.BlockSpec(memory_space=pltpu.VMEM)] * (len(rts) + len(packs) + len(before))
    if scale:
        terms = basis[0].shape[0]
        specs += [pl.BlockSpec(memory_space=pltpu.VMEM)] * len(basis)
        specs.append(pl.BlockSpec(memory_space=pltpu.SMEM))
        scratch.append(pltpu.VMEM((lines, terms), F32))
        shape = [jax.ShapeDtypeStruct((lines // 2, terms), F32)] * 2
        basis = [*basis, core]
    else:
        shape = [jax.ShapeDtypeStruct((own, lines), F32)] * len(rts)
    kernel = functools.partial(value_kernel, plan, len(packs), [i for i, _ in before], scale)
    return pl.pallas_call(
        kernel,
        in_specs=specs,
        out_shape=shape,
        scratch_shapes=scratch,
        compiler_params=params(),
        cost_estimate=pl.CostEstimate(
            flops=1700 * pairs, bytes_accessed=2**20, transcendentals=pairs
        ),
    )(*rts, *packs, *[v for _, v in before], *basis)


def picks_of(exps):
    count = exps.shape[1]
    e = exps[...].astype(F32)
    row = lax.broadcasted_iota(jnp.int32, (count, count), 0)
    col = lax.broadcasted_iota(jnp.int32, (count, count), 1)
    upto = (row <= col).astype(BF)
    cum = jnp.dot(e.astype(BF), upto, preferred_element_type=F32)
    before = cum - e
    picks = [
        jnp.where((cum > t + 0.5) & (before < t + 0.5), 1.0, 0.0).astype(BF) for t in range(3)
    ]
    return [jnp.concatenate([p, p], axis=1) for p in picks]


def basis_kernel(exps, scens, high, low, rt):
    factors = rt.shape[1] // 2
    r = scens[:factors, :].astype(F32).T.astype(BF)
    rt[:, :factors] = r
    rt[:, factors:] = r
    picks = picks_of(exps)
    for c in range(0, scens.shape[1], CHUNK):
        part = scens[factors:, c : c + CHUNK]
        x = [jnp.dot(p, part, preferred_element_type=F32) for p in picks]
        b = x[0] * x[1] * x[2]
        h = b.astype(BF)
        high[:, c : c + CHUNK] = h
        low[:, c : c + CHUNK] = (b - h.astype(F32)).astype(BF)


def first_kernel(exps, scens, p0, p1, high, low, rt, out, w, oh, lev):
    basis_kernel(exps, scens, high, low, rt)
    value_kernel([None], 2, (), None, rt, p0, p1, out, w, oh, lev)


def gram_kernel(start, exps, scens, first, high, low, rt, keep, send):
    basis_kernel(exps, scens, high, low, rt)
    rows = keep.shape[0]
    for i, out in enumerate((keep, send)):
        r0 = pl.multiple_of(start[i] * rows, rows)
        out[...] = lax.dot_general(
            first[pl.ds(r0, rows), :],
            first[...],
            (((1,), (1,)), ((), ())),
            preferred_element_type=F32,
        ) + lax.dot_general(
            high[pl.ds(r0, rows), :],
            high[...],
            (((1,), (1,)), ((), ())),
            preferred_element_type=F32,
        )


def basis_of(exponents, scens, near=(), lines=0, start=None, first=None):
    terms, count = exponents.shape
    factors, own = scens.shape[0] - 2 * count, scens.shape[1]
    shapes = [jax.ShapeDtypeStruct((terms, own), BF)] * 2
    shapes.append(jax.ShapeDtypeStruct((own, 2 * factors), BF))
    vmem = pl.BlockSpec(memory_space=pltpu.VMEM)
    cost = pl.CostEstimate(flops=3 * 10**9, bytes_accessed=3 * 2**20, transcendentals=0)
    if start is None:
        points = near[0].shape[1] * len(near)
        shapes.append(jax.ShapeDtypeStruct((own, lines), F32))
        return pl.pallas_call(
            first_kernel,
            out_shape=shapes,
            scratch_shapes=[
                pltpu.VMEM((2 * factors, points), BF),
                pltpu.VMEM((lines, points), BF),
                pltpu.VMEM((1, points), F32),
            ],
            compiler_params=params(),
            cost_estimate=cost,
        )(exponents, scens, *near)
    shapes += [jax.ShapeDtypeStruct((terms // 4, terms), F32)] * 2
    return pl.pallas_call(
        gram_kernel,
        in_specs=[pl.BlockSpec(memory_space=pltpu.SMEM)] + [vmem] * 3,
        out_shape=shapes,
        compiler_params=params(),
        cost_estimate=cost,
    )(start, exponents, scens, first)


def place_kernel(blocks, *refs):
    order, pieces, out = refs[0], refs[1:-1], refs[-1]
    rows = out.shape[0] // blocks
    k = 0
    for piece in pieces:
        for i in range(piece.shape[0] // rows):
            at = pl.multiple_of(order[k] * rows, rows)
            out[pl.ds(at, rows), :] = piece[i * rows : (i + 1) * rows, :]
            k += 1


def placed(blocks, order, pieces, terms):
    return pl.pallas_call(
        functools.partial(place_kernel, blocks),
        in_specs=[pl.BlockSpec(memory_space=pltpu.SMEM)]
        + [pl.BlockSpec(memory_space=pltpu.VMEM)] * len(pieces),
        out_shape=jax.ShapeDtypeStruct((terms, terms), F32),
        compiler_params=params(),
        cost_estimate=pl.CostEstimate(
            flops=2**20, bytes_accessed=2 * 2**20, transcendentals=0
        ),
    )(order, *pieces)


def after(x, done):
    return lax.optimization_barrier((x, done))[0]


def local(n, returns, exposures, guarantees, guar_type, line_ids, drivers, exponents):
    lines = LINES
    scen_total = returns.shape[1] * n
    all_points = exposures.shape[0] * n
    terms = exponents.shape[0]
    me = lax.axis_index("scen").astype(jnp.int32)
    core, side = me & 1, (me >> 1) & 1

    def swap(x, mask):
        return lax.ppermute(x, "scen", [(i, i ^ mask) for i in range(n)])

    far = list(range(4, n, 4))
    deep = [4 << i for i in range((n // 4).bit_length() - 1)]
    scale = 1.0 / (math.sqrt(all_points / lines) * scen_total)
    pack, scens0 = packs_of(exposures, guarantees, guar_type, line_ids, returns, drivers)

    near = (pack, swap(pack, 1))
    scens1 = swap(scens0, 2)
    packs = {m: swap(pack, m) for m in deep}

    high0, low0, rt0, v = basis_of(exponents, scens0, near, lines)
    before = [(0, v)]
    packs = {m: after(p, v) for m, p in packs.items()}
    for m in far:
        top = max(h for h in deep if h <= m)
        if m not in packs:
            packs[m] = swap(packs[m ^ top], top)

    base = side * 2 + core
    start = jnp.stack([base, base ^ 1])
    high1, low1, rt1, keep, send = basis_of(
        exponents, after(scens1, v), start=start, first=high0
    )
    more = swap(send, 1)
    (v,) = values_of([rt1], near, [None], lines)
    before.append((1, v))
    keep, more = after((keep, more), v)
    gram = (keep + more) * (1.0 / scen_total)

    rts = [rt0, rt1]
    steps = list(deep)
    for i, m in enumerate(far):
        pair = [packs[m], swap(after(packs[m], v), 1)]
        if steps:
            mine = gram.astype(HALF)
            other = swap(mine, steps.pop(0))
        if m == far[-1]:
            break
        v0, v1 = values_of(rts, after(pair, gram), [None, None], lines)
        before += [(0, v0), (1, v1)]
        if i > 0:
            v = v0
        if steps:
            gram = mine.astype(F32) + after(other, v0).astype(F32)
        else:
            gram = after(gram, v0)
    basis = (high0, low0, high1, low1)
    keep, send = values_of(
        rts, after(pair, gram), [None, None], lines, before, basis, scale, core.reshape(1)
    )

    a = (mine.astype(F32) + after(other, keep).astype(F32)).astype(HALF)
    b = swap(a, 2)
    rhs = keep + swap(send, 1)
    for m in [2] + deep:
        mine = rhs.astype(HALF)
        other = swap(mine, m)
        if m == deep[-1]:
            c = swap(jnp.concatenate([a, b], axis=0), 1)
            order = jnp.stack([base ^ k for k in (0, 2, 1, 3)])
            gram = placed(4, order, [x.astype(F32) for x in (a, b, c)], terms)
            other = after(other, gram)
        rhs = mine.astype(F32) + other.astype(F32)
        if m == 2:
            b = after(b, rhs)
    other = swap(rhs, 1)
    first = jnp.where(core == 0, rhs, other)
    second = jnp.where(core == 0, other, rhs)
    return (gram, jnp.concatenate([first, second], axis=0).T)


def solution(mesh):
    spots = (
        P(None, ("grp", "scen")),
        P(("grp", "scen"), None),
        P(("grp", "scen")),
        P(("grp", "scen")),
        P(("grp", "scen")),
        P(None, ("grp", "scen")),
        P(),
    )
    return jax.shard_map(
        functools.partial(local, mesh.shape["scen"]),
        mesh=mesh,
        in_specs=spots,
        out_specs=(P("grp", None), P("grp", None)),
        check_vma=False,
    )
```

```python
import functools
import math

import jax
import jax.numpy as jnp
from jax import lax
from jax.experimental import pallas as pl
from jax.experimental.pallas import tpu as pltpu
from jax.sharding import PartitionSpec as P

LINES = 64
TAIL = 16
CHUNK = 512
LOG2E = 1.4426950408889634
BF = jnp.bfloat16
F32 = jnp.float32
HALF = jnp.float16
VMEM = 24 * 2**20


def params(limit=VMEM):
    return pltpu.CompilerParams(vmem_limit_bytes=limit)


def parts_of(x, count):
    parts = []
    for _ in range(count):
        parts.append(x.astype(BF).astype(F32))
        x = x - parts[-1]
    return parts


def pack_kernel(*refs):
    points, scens = refs[6:8]
    held, sems = refs[8:14], refs[14]
    loads = [pltpu.make_async_copy(refs[i], held[i], sems.at[i]) for i in range(6)]
    for load in loads:
        load.start()
    for load in loads:
        load.wait()
    exposures, guarantees, kinds, lines, returns, drivers = held
    factors = exposures.shape[0]
    points[:factors, :] = exposures[...]
    level = guarantees[...] * (1.0 + 0.15 * kinds[...].astype(F32))
    rows = [*parts_of(level, 3), lines[...].astype(F32)]
    rows.append(jnp.zeros((TAIL - 4, level.shape[1]), F32))
    points[factors:, :] = jnp.concatenate(rows, axis=0).astype(BF)
    scens[:factors, :] = returns[...]
    scens[factors:, :] = jnp.concatenate(parts_of(drivers[...], 2), axis=0).astype(BF)


def packs_of(exposures, guarantees, kinds, lines, returns, drivers):
    points, factors = exposures.shape
    row = (1, points)
    args = (
        exposures.T,
        guarantees.reshape(row),
        kinds.reshape(row),
        lines.reshape(row),
        returns,
        drivers,
    )
    return pl.pallas_call(
        pack_kernel,
        in_specs=[pl.BlockSpec(memory_space=pltpu.HBM)] * len(args),
        out_shape=[
            jax.ShapeDtypeStruct((factors + TAIL, points), BF),
            jax.ShapeDtypeStruct((factors + 2 * drivers.shape[0], returns.shape[1]), BF),
        ],
        scratch_shapes=[pltpu.VMEM(a.shape, a.dtype) for a in args]
        + [pltpu.SemaphoreType.DMA((len(args),))],
        compiler_params=params(58 * 2**20),
        cost_estimate=pl.CostEstimate(flops=2**20, bytes_accessed=2**20, transcendentals=0),
    )(*args)


def prepare(packs, w, oh, lev):
    factors = w.shape[0] // 2
    points = packs[0].shape[1]
    for i, pack in enumerate(packs):
        at = slice(i * points, (i + 1) * points)
        e = pack[:factors, :].astype(F32) * LOG2E
        high = e.astype(BF)
        w[:factors, at] = high
        w[factors:, at] = (e - high.astype(F32)).astype(BF)
        tail = pack[factors:, :].astype(F32)
        lev[:, at] = tail[0:1] + tail[1:2] + tail[2:3]
        label = lax.broadcasted_iota(jnp.int32, (oh.shape[0], points), 0).astype(F32)
        oh[:, at] = (label == tail[3:4]).astype(BF)


def chunk_values(r, w, oh, lev, step):
    total = None
    for j in range(0, w.shape[1], step):
        at = slice(j, j + step)
        power = jnp.dot(r, w[:, at], preferred_element_type=F32)
        payoff = jnp.maximum(lev[:, at] - jnp.exp2(power), 0.0).astype(BF)
        part = lax.dot_general(
            payoff, oh[:, at], (((1,), (1,)), ((), ())), preferred_element_type=F32
        )
        total = part if total is None else total + part
    return total


def value_kernel(blocks, count, earlier, scale, *refs):
    rts, refs = refs[:blocks], refs[blocks:]
    packs, refs = refs[:count], refs[count:]
    sources = list(rts)
    if scale:
        before, refs = refs[: len(earlier)], refs[len(earlier) :]
        basis, refs = refs[: 2 * blocks], refs[2 * blocks :]
        core, keep, send, w, oh, lev, sems, *held = refs
        whole, held = held[0], held[1:]
        sources += [*before, *basis]
    else:
        outs, (w, oh, lev, sems, *held) = refs[:blocks], refs[blocks:]
        sums, held = held[:blocks], held[blocks:]
    loads = [pltpu.make_async_copy(a, b, sems.at[i]) for i, (a, b) in enumerate(zip(sources, held))]
    for load in loads:
        load.start()
    own, double = rts[0].shape
    points = packs[0].shape[1]
    prepare(packs, w, oh, lev)
    for load in loads[:blocks]:
        load.wait()
    totals = [
        [
            chunk_values(held[i][s0 : s0 + CHUNK, :], w, oh, lev, points)
            for s0 in range(0, own, CHUNK)
        ]
        for i in range(blocks)
    ]
    if not scale:
        stores = []
        for i in range(blocks):
            sums[i][...] = jnp.concatenate(totals[i], axis=0)
            stores.append(pltpu.make_async_copy(sums[i], outs[i], sems.at[len(sources) + i]))
            stores[-1].start()
        for store in stores:
            store.wait()
        return
    for load in loads[blocks:]:
        load.wait()
    before, basis = held[blocks : blocks + len(before)], held[blocks + len(before) :]
    lines = oh.shape[0]
    result = None
    for i in range(blocks):
        v = jnp.concatenate(totals[i], axis=0)
        for k, at in enumerate(earlier):
            if at == i:
                v = v + before[k][...]
        vh = v.astype(BF)
        vl = (v - vh.astype(F32)).astype(BF)
        both = jnp.concatenate([vh, vl], axis=1)
        a = jnp.dot(basis[2 * i][...], both, preferred_element_type=F32)
        b = jnp.dot(basis[2 * i + 1][...], vh, preferred_element_type=F32)
        part = a[:, :lines] + a[:, lines:] + b
        result = part if result is None else result + part
    whole[...] = (result * scale).T
    half = lines // 2
    keep[...] = whole[pl.ds(pl.multiple_of(core[0] * half, half), half), :]
    send[...] = whole[pl.ds(pl.multiple_of((1 - core[0]) * half, half), half), :]


VSPEC = pl.BlockSpec(memory_space=pltpu.VMEM)
SSPEC = pl.BlockSpec(memory_space=pltpu.SMEM)
HSPEC = pl.BlockSpec(memory_space=pltpu.HBM)


def like(arrays):
    return [pltpu.VMEM(a.shape, a.dtype) for a in arrays]


def point_scratch(double, lines, points):
    return [
        pltpu.VMEM((double, points), BF),
        pltpu.VMEM((lines, points), BF),
        pltpu.VMEM((1, points), F32),
    ]


def values_of(rts, packs, lines, before=(), basis=(), scale=None, core=None):
    own, double = rts[0].shape
    points = packs[0].shape[1]
    pairs = own * points * len(rts) * len(packs)
    held = [*rts, *[v for _, v in before], *basis]
    scratch = point_scratch(double, lines, points * len(packs))
    scratch.append(pltpu.SemaphoreType.DMA((len(held) + len(rts),)))
    specs = [HSPEC] * len(rts) + [VSPEC] * len(packs)
    if scale:
        terms = basis[0].shape[0]
        specs += [HSPEC] * (len(before) + len(basis)) + [SSPEC]
        scratch.append(pltpu.VMEM((lines, terms), F32))
        shape = [jax.ShapeDtypeStruct((lines // 2, terms), F32)] * 2
        outs = [VSPEC] * 2
        basis = [*basis, core]
    else:
        shape = [jax.ShapeDtypeStruct((own, lines), F32)] * len(rts)
        outs = [HSPEC] * len(rts)
        scratch += like(shape)
    kernel = functools.partial(value_kernel, len(rts), len(packs), [i for i, _ in before], scale)
    return pl.pallas_call(
        kernel,
        in_specs=specs,
        out_specs=outs,
        out_shape=shape,
        scratch_shapes=scratch + like(held),
        compiler_params=params(),
        cost_estimate=pl.CostEstimate(
            flops=1700 * pairs, bytes_accessed=2**20, transcendentals=pairs
        ),
    )(*rts, *packs, *[v for _, v in before], *basis)


def picks_of(exps):
    count = exps.shape[1]
    e = exps[...].astype(F32)
    row = lax.broadcasted_iota(jnp.int32, (count, count), 0)
    col = lax.broadcasted_iota(jnp.int32, (count, count), 1)
    upto = (row <= col).astype(BF)
    cum = jnp.dot(e.astype(BF), upto, preferred_element_type=F32)
    before = cum - e
    picks = [
        jnp.where((cum > t + 0.5) & (before < t + 0.5), 1.0, 0.0).astype(BF) for t in range(3)
    ]
    return [jnp.concatenate([p, p], axis=1) for p in picks]


def basis_kernel(exps, scens, high, low, rt):
    factors = rt.shape[1] // 2
    r = scens[:factors, :].astype(F32).T.astype(BF)
    rt[:, :factors] = r
    rt[:, factors:] = r
    picks = picks_of(exps)
    for c in range(0, scens.shape[1], CHUNK):
        part = scens[factors:, c : c + CHUNK]
        x = [jnp.dot(p, part, preferred_element_type=F32) for p in picks]
        b = x[0] * x[1] * x[2]
        h = b.astype(BF)
        high[:, c : c + CHUNK] = h
        low[:, c : c + CHUNK] = (b - h.astype(F32)).astype(BF)


def first_kernel(exps, scens, p0, p1, *refs):
    outs, (w, oh, lev, sems, packs, *held) = refs[:4], refs[4:]
    loads = [pltpu.make_async_copy(p, packs.at[i], sems.at[4 + i]) for i, p in enumerate((p0, p1))]
    for load in loads:
        load.start()
    stores = [pltpu.make_async_copy(a, b, sems.at[i]) for i, (a, b) in enumerate(zip(held, outs))]
    basis_kernel(exps, scens, *held[:3])
    for store in stores[:3]:
        store.start()
    for load in loads:
        load.wait()
    prepare([packs.at[0], packs.at[1]], w, oh, lev)
    points = packs.shape[2]
    for s0 in range(0, held[2].shape[0], CHUNK):
        held[3][s0 : s0 + CHUNK, :] = chunk_values(
            held[2][s0 : s0 + CHUNK, :], w, oh, lev, points
        )
    stores[3].start()
    for store in stores:
        store.wait()


def gram_kernel(start, exps, scens, earlier, *refs):
    outs, keep, send, (sems, first, *held) = refs[:3], refs[3], refs[4], refs[5:]
    load = pltpu.make_async_copy(earlier, first, sems.at[3])
    load.start()
    stores = [pltpu.make_async_copy(a, b, sems.at[i]) for i, (a, b) in enumerate(zip(held, outs))]
    high = held[0]
    basis_kernel(exps, scens, *held)
    for store in stores:
        store.start()
    load.wait()
    rows = keep.shape[0]
    for i, out in enumerate((keep, send)):
        r0 = pl.multiple_of(start[i] * rows, rows)
        total = None
        for b in (first, high):
            part = lax.dot_general(
                b[pl.ds(r0, rows), :], b[...], (((1,), (1,)), ((), ())), preferred_element_type=F32
            )
            total = part if total is None else total + part
        out[...] = total
    for store in stores:
        store.wait()


def basis_of(exponents, scens, near=(), lines=0, start=None, first=None):
    terms, count = exponents.shape
    factors, own = scens.shape[0] - 2 * count, scens.shape[1]
    shapes = [jax.ShapeDtypeStruct((terms, own), BF)] * 2
    shapes.append(jax.ShapeDtypeStruct((own, 2 * factors), BF))
    cost = pl.CostEstimate(flops=3 * 10**9, bytes_accessed=3 * 2**20, transcendentals=0)
    if start is None:
        points = near[0].shape[1]
        shapes.append(jax.ShapeDtypeStruct((own, lines), F32))
        return pl.pallas_call(
            first_kernel,
            in_specs=[VSPEC] * 2 + [HSPEC] * 2,
            out_specs=[HSPEC] * 4,
            out_shape=shapes,
            scratch_shapes=point_scratch(2 * factors, lines, 2 * points)
            + [pltpu.SemaphoreType.DMA((6,)), pltpu.VMEM((2, *near[0].shape), BF)]
            + like(shapes),
            compiler_params=params(),
            cost_estimate=cost,
        )(exponents, scens, *near)
    scratch = [pltpu.SemaphoreType.DMA((4,)), *like([first]), *like(shapes)]
    shapes += [jax.ShapeDtypeStruct((terms // 4, terms), F32)] * 2
    return pl.pallas_call(
        gram_kernel,
        in_specs=[SSPEC, VSPEC, VSPEC, HSPEC],
        out_specs=[HSPEC] * 3 + [VSPEC] * 2,
        out_shape=shapes,
        scratch_shapes=scratch,
        compiler_params=params(),
        cost_estimate=cost,
    )(start, exponents, scens, first)


def place_kernel(blocks, *refs):
    order, pieces, out = refs[0], refs[1:-1], refs[-1]
    rows = out.shape[0] // blocks
    k = 0
    for piece in pieces:
        for i in range(piece.shape[0] // rows):
            at = pl.multiple_of(order[k] * rows, rows)
            out[pl.ds(at, rows), :] = piece[i * rows : (i + 1) * rows, :]
            k += 1


def placed(blocks, order, pieces, terms):
    return pl.pallas_call(
        functools.partial(place_kernel, blocks),
        in_specs=[pl.BlockSpec(memory_space=pltpu.SMEM)]
        + [pl.BlockSpec(memory_space=pltpu.VMEM)] * len(pieces),
        out_shape=jax.ShapeDtypeStruct((terms, terms), F32),
        compiler_params=params(),
        cost_estimate=pl.CostEstimate(
            flops=2**20, bytes_accessed=2 * 2**20, transcendentals=0
        ),
    )(order, *pieces)


def after(x, done):
    return lax.optimization_barrier((x, done))[0]


def local(n, returns, exposures, guarantees, guar_type, line_ids, drivers, exponents):
    lines = LINES
    scen_total = returns.shape[1] * n
    all_points = exposures.shape[0] * n
    terms = exponents.shape[0]
    me = lax.axis_index("scen").astype(jnp.int32)
    core, side = me & 1, (me >> 1) & 1

    def swap(x, mask):
        return lax.ppermute(x, "scen", [(i, i ^ mask) for i in range(n)])

    far = list(range(4, n, 4))
    deep = [4 << i for i in range((n // 4).bit_length() - 1)]
    scale = 1.0 / (math.sqrt(all_points / lines) * scen_total)
    pack, scens0 = packs_of(exposures, guarantees, guar_type, line_ids, returns, drivers)

    near = (pack, swap(pack, 1))
    scens1 = swap(scens0, 2)
    packs = {m: swap(pack, m) for m in deep}

    high0, low0, rt0, v = basis_of(exponents, scens0, near, lines)
    before = [(0, v)]
    packs[4] = after(packs[4], v)
    for m in far:
        top = max(h for h in deep if h <= m)
        if m not in packs:
            packs[m] = swap(packs[m ^ top], top)

    base = side * 2 + core
    start = jnp.stack([base, base ^ 1])
    high1, low1, rt1, keep, send = basis_of(
        exponents, after(scens1, v), start=start, first=high0
    )
    more = swap(send, 1)
    (v,) = values_of([rt1], near, lines)
    before.append((1, v))
    keep, more = after((keep, more), v)
    gram = (keep + more) * (1.0 / scen_total)

    rts = [rt0, rt1]
    steps = list(deep)
    for i, m in enumerate(far):
        pair = [packs[m], swap(after(packs[m], v), 1)]
        if steps:
            mine = gram.astype(HALF)
            other = swap(mine, steps.pop(0))
        if m == far[-1]:
            break
        v0, v1 = values_of(rts, after(pair, gram), lines)
        before += [(0, v0), (1, v1)]
        if i > 0:
            v = v0
        if other is not None:
            gram = mine.astype(F32) + after(other, v0).astype(F32)
            other = None
        else:
            gram = after(gram, v0)
    basis = (high0, low0, high1, low1)
    keep, send = values_of(
        rts, after(pair, gram), lines, before, basis, scale, core.reshape(1)
    )

    a = after(gram, keep).astype(HALF)
    b = swap(a, 2)
    rhs = keep + swap(send, 1)
    for m in [2] + deep:
        mine = rhs.astype(HALF)
        other = swap(mine, m)
        if m == deep[-1]:
            c = swap(jnp.concatenate([a, b], axis=0), 1)
            order = jnp.stack([base ^ k for k in (0, 2, 1, 3)])
            gram = placed(4, order, [x.astype(F32) for x in (a, b, c)], terms)
            other = after(other, gram)
        rhs = mine.astype(F32) + other.astype(F32)
        if m == 2:
            b = after(b, rhs)
    other = swap(rhs, 1)
    first = jnp.where(core == 0, rhs, other)
    second = jnp.where(core == 0, other, rhs)
    return (gram, jnp.concatenate([first, second], axis=0).T)


def solution(mesh):
    spots = (
        P(None, ("grp", "scen")),
        P(("grp", "scen"), None),
        P(("grp", "scen")),
        P(("grp", "scen")),
        P(("grp", "scen")),
        P(None, ("grp", "scen")),
        P(),
    )
    return jax.shard_map(
        functools.partial(local, mesh.shape["scen"]),
        mesh=mesh,
        in_specs=spots,
        out_specs=(P("grp", None), P("grp", None)),
        check_vma=False,
    )
```

```python
import functools
import math

import jax
import jax.numpy as jnp
from jax import lax
from jax.experimental import pallas as pl
from jax.experimental.pallas import tpu as pltpu
from jax.sharding import PartitionSpec as P

LINES = 64
TAIL = 16
CHUNK = 512
LOG2E = 1.4426950408889634
BF = jnp.bfloat16
F32 = jnp.float32
HALF = jnp.float16
VMEM = 24 * 2**20


def params(limit=VMEM):
    return pltpu.CompilerParams(vmem_limit_bytes=limit)


def parts_of(x, count):
    parts = []
    for _ in range(count):
        parts.append(x.astype(BF).astype(F32))
        x = x - parts[-1]
    return parts


def pack_kernel(*refs):
    points, scens = refs[6:8]
    held, sems = refs[8:14], refs[14]
    loads = [pltpu.make_async_copy(refs[i], held[i], sems.at[i]) for i in range(6)]
    for load in loads:
        load.start()
    for load in loads:
        load.wait()
    exposures, guarantees, kinds, lines, returns, drivers = held
    factors = exposures.shape[0]
    points[:factors, :] = exposures[...]
    level = guarantees[...] * (1.0 + 0.15 * kinds[...].astype(F32))
    rows = [*parts_of(level, 3), lines[...].astype(F32)]
    rows.append(jnp.zeros((TAIL - 4, level.shape[1]), F32))
    points[factors:, :] = jnp.concatenate(rows, axis=0).astype(BF)
    scens[:factors, :] = returns[...]
    scens[factors:, :] = jnp.concatenate(parts_of(drivers[...], 2), axis=0).astype(BF)


def packs_of(exposures, guarantees, kinds, lines, returns, drivers):
    points, factors = exposures.shape
    row = (1, points)
    args = (
        exposures.T,
        guarantees.reshape(row),
        kinds.reshape(row),
        lines.reshape(row),
        returns,
        drivers,
    )
    return pl.pallas_call(
        pack_kernel,
        in_specs=[pl.BlockSpec(memory_space=pltpu.HBM)] * len(args),
        out_shape=[
            jax.ShapeDtypeStruct((factors + TAIL, points), BF),
            jax.ShapeDtypeStruct((factors + 2 * drivers.shape[0], returns.shape[1]), BF),
        ],
        scratch_shapes=[pltpu.VMEM(a.shape, a.dtype) for a in args]
        + [pltpu.SemaphoreType.DMA((len(args),))],
        compiler_params=params(58 * 2**20),
        cost_estimate=pl.CostEstimate(flops=2**20, bytes_accessed=2**20, transcendentals=0),
    )(*args)


def prepare(packs, w, oh, lev):
    factors = w.shape[0] // 2
    points = packs[0].shape[1]
    for i, pack in enumerate(packs):
        at = slice(i * points, (i + 1) * points)
        e = pack[:factors, :].astype(F32) * LOG2E
        high = e.astype(BF)
        w[:factors, at] = high
        w[factors:, at] = (e - high.astype(F32)).astype(BF)
        tail = pack[factors:, :].astype(F32)
        lev[:, at] = tail[0:1] + tail[1:2] + tail[2:3]
        label = lax.broadcasted_iota(jnp.int32, (oh.shape[0], points), 0).astype(F32)
        oh[:, at] = (label == tail[3:4]).astype(BF)


def chunk_values(r, w, oh, lev, step):
    total = None
    for j in range(0, w.shape[1], step):
        at = slice(j, j + step)
        power = jnp.dot(r, w[:, at], preferred_element_type=F32)
        payoff = jnp.maximum(lev[:, at] - jnp.exp2(power), 0.0).astype(BF)
        part = lax.dot_general(
            payoff, oh[:, at], (((1,), (1,)), ((), ())), preferred_element_type=F32
        )
        total = part if total is None else total + part
    return total


def value_kernel(blocks, count, earlier, scale, *refs):
    rts, refs = refs[:blocks], refs[blocks:]
    packs, refs = refs[:count], refs[count:]
    before, refs = refs[:earlier], refs[earlier:]
    sources = [*rts, *before]
    if scale:
        basis, refs = refs[: 2 * blocks], refs[2 * blocks :]
        out, w, oh, lev, sems, *held = refs
        sources += basis
    else:
        out, w, oh, lev, sems, sums, *held = refs
    loads = [pltpu.make_async_copy(a, b, sems.at[i]) for i, (a, b) in enumerate(zip(sources, held))]
    for load in loads:
        load.start()
    own = rts[0].shape[0]
    points = packs[0].shape[1]
    lines = oh.shape[0]
    prepare(packs, w, oh, lev)
    for load in loads[:blocks]:
        load.wait()
    totals = [
        [
            chunk_values(held[i][s0 : s0 + CHUNK, :], w, oh, lev, points)
            for s0 in range(0, own, CHUNK)
        ]
        for i in range(blocks)
    ]
    for load in loads[blocks:]:
        load.wait()
    before, basis = held[blocks : blocks + earlier], held[blocks + earlier :]
    totals = [jnp.concatenate(t, axis=0) for t in totals]
    if not scale:
        sums[:, :lines] = totals[0] + before[0][:, :lines]
        sums[:, lines:] = totals[1] + before[-1][:, -lines:]
        store = pltpu.make_async_copy(sums, out, sems.at[len(sources)])
        store.start()
        store.wait()
        return
    result = None
    for i in range(blocks):
        v = totals[i] + before[0][:, i * lines : (i + 1) * lines]
        vh = v.astype(BF)
        vl = (v - vh.astype(F32)).astype(BF)
        both = jnp.concatenate([vh, vl], axis=1)
        a = jnp.dot(basis[2 * i][...], both, preferred_element_type=F32)
        b = jnp.dot(basis[2 * i + 1][...], vh, preferred_element_type=F32)
        part = a[:, :lines] + a[:, lines:] + b
        result = part if result is None else result + part
    out[...] = (result * scale).T


def plain_kernel(rt, *refs):
    packs, (out, w, oh, lev, sems, sums, held) = refs[:-7], refs[-7:]
    load = pltpu.make_async_copy(rt, held, sems.at[0])
    load.start()
    prepare(packs, w, oh, lev)
    load.wait()
    for s0 in range(0, rt.shape[0], CHUNK):
        sums[s0 : s0 + CHUNK, :] = chunk_values(
            held[s0 : s0 + CHUNK, :], w, oh, lev, packs[0].shape[1]
        )
    store = pltpu.make_async_copy(sums, out, sems.at[1])
    store.start()
    store.wait()


VSPEC = pl.BlockSpec(memory_space=pltpu.VMEM)
SSPEC = pl.BlockSpec(memory_space=pltpu.SMEM)
HSPEC = pl.BlockSpec(memory_space=pltpu.HBM)


def like(arrays):
    return [pltpu.VMEM(a.shape, a.dtype) for a in arrays]


def point_scratch(double, lines, points):
    return [
        pltpu.VMEM((double, points), BF),
        pltpu.VMEM((lines, points), BF),
        pltpu.VMEM((1, points), F32),
    ]


def values_of(rts, packs, lines, before=(), basis=(), scale=None):
    own, double = rts[0].shape
    points = packs[0].shape[1]
    pairs = own * points * len(rts) * len(packs)
    held = [*rts, *before, *basis]
    scratch = point_scratch(double, lines, points * len(packs))
    scratch.append(pltpu.SemaphoreType.DMA((len(held) + 1,)))
    kernel = functools.partial(value_kernel, len(rts), len(packs), len(before), scale)
    out = HSPEC
    if scale:
        shape = jax.ShapeDtypeStruct((lines, basis[0].shape[0]), F32)
        out = VSPEC
    else:
        shape = jax.ShapeDtypeStruct((own, lines * len(rts)), F32)
        scratch += like([shape])
    if not before:
        kernel = plain_kernel
    return pl.pallas_call(
        kernel,
        in_specs=[HSPEC] * len(rts)
        + [VSPEC] * len(packs)
        + [HSPEC] * (len(before) + len(basis)),
        out_specs=out,
        out_shape=shape,
        scratch_shapes=scratch + like(held),
        compiler_params=params(),
        cost_estimate=pl.CostEstimate(
            flops=1700 * pairs, bytes_accessed=2**20, transcendentals=pairs
        ),
    )(*rts, *packs, *before, *basis)


def picks_of(exps):
    count = exps.shape[1]
    e = exps[...].astype(F32)
    row = lax.broadcasted_iota(jnp.int32, (count, count), 0)
    col = lax.broadcasted_iota(jnp.int32, (count, count), 1)
    upto = (row <= col).astype(BF)
    cum = jnp.dot(e.astype(BF), upto, preferred_element_type=F32)
    before = cum - e
    picks = [
        jnp.where((cum > t + 0.5) & (before < t + 0.5), 1.0, 0.0).astype(BF) for t in range(3)
    ]
    return [jnp.concatenate([p, p], axis=1) for p in picks]


def basis_kernel(exps, scens, high, low, rt):
    factors = rt.shape[1] // 2
    r = scens[:factors, :].astype(F32).T.astype(BF)
    rt[:, :factors] = r
    rt[:, factors:] = r
    picks = picks_of(exps)
    for c in range(0, scens.shape[1], CHUNK):
        part = scens[factors:, c : c + CHUNK]
        x = [jnp.dot(p, part, preferred_element_type=F32) for p in picks]
        b = x[0] * x[1] * x[2]
        h = b.astype(BF)
        high[:, c : c + CHUNK] = h
        low[:, c : c + CHUNK] = (b - h.astype(F32)).astype(BF)


def first_kernel(exps, scens, p0, p1, *refs):
    outs, (w, oh, lev, sems, packs, *held) = refs[:4], refs[4:]
    loads = [pltpu.make_async_copy(p, packs.at[i], sems.at[4 + i]) for i, p in enumerate((p0, p1))]
    for load in loads:
        load.start()
    stores = [pltpu.make_async_copy(a, b, sems.at[i]) for i, (a, b) in enumerate(zip(held, outs))]
    basis_kernel(exps, scens, *held[:3])
    for store in stores[:3]:
        store.start()
    for load in loads:
        load.wait()
    prepare([packs.at[0], packs.at[1]], w, oh, lev)
    points = packs.shape[2]
    for s0 in range(0, held[2].shape[0], CHUNK):
        held[3][s0 : s0 + CHUNK, :] = chunk_values(
            held[2][s0 : s0 + CHUNK, :], w, oh, lev, points
        )
    stores[3].start()
    for store in stores:
        store.wait()


def gram_kernel(start, exps, scens, earlier, *refs):
    outs, keep, send, (sems, first, *held) = refs[:3], refs[3], refs[4], refs[5:]
    load = pltpu.make_async_copy(earlier, first, sems.at[3])
    load.start()
    stores = [pltpu.make_async_copy(a, b, sems.at[i]) for i, (a, b) in enumerate(zip(held, outs))]
    high = held[0]
    basis_kernel(exps, scens, *held)
    for store in stores:
        store.start()
    load.wait()
    rows = keep.shape[0]
    for i, out in enumerate((keep, send)):
        r0 = pl.multiple_of(start[i] * rows, rows)
        total = None
        for b in (first, high):
            part = lax.dot_general(
                b[pl.ds(r0, rows), :], b[...], (((1,), (1,)), ((), ())), preferred_element_type=F32
            )
            total = part if total is None else total + part
        out[...] = total
    for store in stores:
        store.wait()


def basis_of(exponents, scens, near=(), lines=0, start=None, first=None):
    terms, count = exponents.shape
    factors, own = scens.shape[0] - 2 * count, scens.shape[1]
    shapes = [jax.ShapeDtypeStruct((terms, own), BF)] * 2
    shapes.append(jax.ShapeDtypeStruct((own, 2 * factors), BF))
    cost = pl.CostEstimate(flops=3 * 10**9, bytes_accessed=3 * 2**20, transcendentals=0)
    if start is None:
        points = near[0].shape[1]
        shapes.append(jax.ShapeDtypeStruct((own, lines), F32))
        return pl.pallas_call(
            first_kernel,
            in_specs=[VSPEC] * 2 + [HSPEC] * 2,
            out_specs=[HSPEC] * 4,
            out_shape=shapes,
            scratch_shapes=point_scratch(2 * factors, lines, 2 * points)
            + [pltpu.SemaphoreType.DMA((6,)), pltpu.VMEM((2, *near[0].shape), BF)]
            + like(shapes),
            compiler_params=params(),
            cost_estimate=cost,
        )(exponents, scens, *near)
    scratch = [pltpu.SemaphoreType.DMA((4,)), *like([first]), *like(shapes)]
    shapes += [jax.ShapeDtypeStruct((terms // 4, terms), F32)] * 2
    return pl.pallas_call(
        gram_kernel,
        in_specs=[SSPEC, VSPEC, VSPEC, HSPEC],
        out_specs=[HSPEC] * 3 + [VSPEC] * 2,
        out_shape=shapes,
        scratch_shapes=scratch,
        compiler_params=params(),
        cost_estimate=cost,
    )(start, exponents, scens, first)


def place_kernel(blocks, *refs):
    order, pieces, out = refs[0], refs[1:-1], refs[-1]
    rows = out.shape[0] // blocks
    k = 0
    for piece in pieces:
        for i in range(piece.shape[0] // rows):
            at = pl.multiple_of(order[k] * rows, rows)
            out[pl.ds(at, rows), :] = piece[i * rows : (i + 1) * rows, :]
            k += 1


def placed(blocks, order, pieces, terms):
    return pl.pallas_call(
        functools.partial(place_kernel, blocks),
        in_specs=[pl.BlockSpec(memory_space=pltpu.SMEM)]
        + [pl.BlockSpec(memory_space=pltpu.VMEM)] * len(pieces),
        out_shape=jax.ShapeDtypeStruct((terms, terms), F32),
        compiler_params=params(),
        cost_estimate=pl.CostEstimate(
            flops=2**20, bytes_accessed=2 * 2**20, transcendentals=0
        ),
    )(order, *pieces)


def after(x, done):
    return lax.optimization_barrier((x, done))[0]


def local(n, returns, exposures, guarantees, guar_type, line_ids, drivers, exponents):
    lines = LINES
    scen_total = returns.shape[1] * n
    all_points = exposures.shape[0] * n
    terms = exponents.shape[0]
    me = lax.axis_index("scen").astype(jnp.int32)
    core, side = me & 1, (me >> 1) & 1

    def swap(x, mask):
        return lax.ppermute(x, "scen", [(i, i ^ mask) for i in range(n)])

    far = list(range(4, n, 4))
    deep = [4 << i for i in range((n // 4).bit_length() - 1)]
    scale = 1.0 / (math.sqrt(all_points / lines) * scen_total)
    pack, scens0 = packs_of(exposures, guarantees, guar_type, line_ids, returns, drivers)

    near = (pack, swap(pack, 1))
    scens1 = swap(scens0, 2)
    packs = {m: swap(pack, m) for m in deep}

    high0, low0, rt0, v = basis_of(exponents, scens0, near, lines)
    before = [v]
    packs[4] = after(packs[4], v)
    for m in far:
        top = max(h for h in deep if h <= m)
        if m not in packs:
            packs[m] = swap(packs[m ^ top], top)

    base = side * 2 + core
    start = jnp.stack([base, base ^ 1])
    high1, low1, rt1, keep, send = basis_of(
        exponents, after(scens1, v), start=start, first=high0
    )
    more = swap(send, 1)
    v = values_of([rt1], near, lines)
    before.append(v)
    keep, more = after((keep, more), v)
    gram = (keep + more) * (1.0 / scen_total)

    rts = [rt0, rt1]
    steps = list(deep)
    for i, m in enumerate(far):
        pair = [packs[m], swap(after(packs[m], v), 1)]
        if steps:
            mine = gram.astype(HALF)
            other = swap(mine, steps.pop(0))
        if m == far[-1]:
            break
        v0 = values_of(rts, after(pair, gram), lines, before)
        before = [v0]
        if i > 0:
            v = v0
        if other is not None:
            gram = mine.astype(F32) + after(other, v0).astype(F32)
            other = None
        else:
            gram = after(gram, v0)
    basis = (high0, low0, high1, low1)
    rhs = values_of(rts, after(pair, gram), lines, before, basis, scale)

    rhs = rhs + swap(rhs, 1)
    for m in [2] + deep:
        mine = rhs.astype(HALF)
        other = swap(mine, m)
        if m == deep[-1]:
            c = swap(jnp.concatenate([a, b], axis=0), 1)
            order = jnp.stack([base ^ k for k in (0, 2, 1, 3)])
            gram = placed(4, order, [x.astype(F32) for x in (a, b, c)], terms)
            other = after(other, gram)
        rhs = mine.astype(F32) + other.astype(F32)
        if m == 2:
            a = after(gram, rhs).astype(HALF)
            b = swap(a, 2)
    return (gram, rhs.T)


def solution(mesh):
    spots = (
        P(None, ("grp", "scen")),
        P(("grp", "scen"), None),
        P(("grp", "scen")),
        P(("grp", "scen")),
        P(("grp", "scen")),
        P(None, ("grp", "scen")),
        P(),
    )
    return jax.shard_map(
        functools.partial(local, mesh.shape["scen"]),
        mesh=mesh,
        in_specs=spots,
        out_specs=(P("grp", None), P("grp", None)),
        check_vma=False,
    )
```

```python
import functools
import math

import jax
import jax.numpy as jnp
from jax import lax
from jax.experimental import pallas as pl
from jax.experimental.pallas import tpu as pltpu
from jax.sharding import PartitionSpec as P

LINES = 64
TAIL = 16
CHUNK = 512
LOG2E = 1.4426950408889634
BF = jnp.bfloat16
F32 = jnp.float32
HALF = jnp.float16
VMEM = 24 * 2**20


def params(limit=VMEM):
    return pltpu.CompilerParams(vmem_limit_bytes=limit)


def parts_of(x, count):
    parts = []
    for _ in range(count):
        parts.append(x.astype(BF).astype(F32))
        x = x - parts[-1]
    return parts


def pack_kernel(*refs):
    points, scens = refs[6:8]
    held, sems = refs[8:14], refs[14]
    loads = [pltpu.make_async_copy(refs[i], held[i], sems.at[i]) for i in range(6)]
    for load in loads:
        load.start()
    for load in loads:
        load.wait()
    exposures, guarantees, kinds, lines, returns, drivers = held
    factors = exposures.shape[0]
    points[:factors, :] = exposures[...]
    level = guarantees[...] * (1.0 + 0.15 * kinds[...].astype(F32))
    rows = [*parts_of(level, 3), lines[...].astype(F32)]
    rows.append(jnp.zeros((TAIL - 4, level.shape[1]), F32))
    points[factors:, :] = jnp.concatenate(rows, axis=0).astype(BF)
    scens[:factors, :] = returns[...]
    scens[factors:, :] = jnp.concatenate(parts_of(drivers[...], 2), axis=0).astype(BF)


def packs_of(exposures, guarantees, kinds, lines, returns, drivers):
    points, factors = exposures.shape
    row = (1, points)
    args = (
        exposures.T,
        guarantees.reshape(row),
        kinds.reshape(row),
        lines.reshape(row),
        returns,
        drivers,
    )
    return pl.pallas_call(
        pack_kernel,
        in_specs=[pl.BlockSpec(memory_space=pltpu.HBM)] * len(args),
        out_shape=[
            jax.ShapeDtypeStruct((factors + TAIL, points), BF),
            jax.ShapeDtypeStruct((factors + 2 * drivers.shape[0], returns.shape[1]), BF),
        ],
        scratch_shapes=[pltpu.VMEM(a.shape, a.dtype) for a in args]
        + [pltpu.SemaphoreType.DMA((len(args),))],
        compiler_params=params(58 * 2**20),
        cost_estimate=pl.CostEstimate(flops=2**20, bytes_accessed=2**20, transcendentals=0),
    )(*args)


def prepare(packs, w, oh, lev):
    factors = w.shape[0] // 2
    points = packs[0].shape[1]
    for i, pack in enumerate(packs):
        at = slice(i * points, (i + 1) * points)
        e = pack[:factors, :].astype(F32) * LOG2E
        high = e.astype(BF)
        w[:factors, at] = high
        w[factors:, at] = (e - high.astype(F32)).astype(BF)
        tail = pack[factors:, :].astype(F32)
        lev[:, at] = tail[0:1] + tail[1:2] + tail[2:3]
        label = lax.broadcasted_iota(jnp.int32, (oh.shape[0], points), 0).astype(F32)
        oh[:, at] = (label == tail[3:4]).astype(BF)


def chunk_values(r, w, oh, lev, step):
    total = None
    for j in range(0, w.shape[1], step):
        at = slice(j, j + step)
        power = jnp.dot(r, w[:, at], preferred_element_type=F32)
        payoff = jnp.maximum(lev[:, at] - jnp.exp2(power), 0.0).astype(BF)
        part = lax.dot_general(
            payoff, oh[:, at], (((1,), (1,)), ((), ())), preferred_element_type=F32
        )
        total = part if total is None else total + part
    return total


def value_kernel(blocks, count, earlier, scale, *refs):
    rts, refs = refs[:blocks], refs[blocks:]
    packs, refs = refs[:count], refs[count:]
    before, refs = refs[:earlier], refs[earlier:]
    sources = [*rts, *before]
    if scale:
        basis, refs = refs[: 2 * blocks], refs[2 * blocks :]
        out, w, oh, lev, sems, *held = refs
        sources += basis
    else:
        out, w, oh, lev, sems, sums, *held = refs
    loads = [pltpu.make_async_copy(a, b, sems.at[i]) for i, (a, b) in enumerate(zip(sources, held))]
    for load in loads:
        load.start()
    own = rts[0].shape[0]
    points = packs[0].shape[1]
    lines = oh.shape[0]
    prepare(packs, w, oh, lev)
    for load in loads[:blocks]:
        load.wait()
    totals = [
        [
            chunk_values(held[i][s0 : s0 + CHUNK, :], w, oh, lev, points)
            for s0 in range(0, own, CHUNK)
        ]
        for i in range(blocks)
    ]
    for load in loads[blocks:]:
        load.wait()
    before, basis = held[blocks : blocks + earlier], held[blocks + earlier :]
    totals = [jnp.concatenate(t, axis=0) for t in totals]
    if not scale:
        sums[:, :lines] = totals[0] + before[0][:, :lines]
        sums[:, lines:] = totals[1] + before[-1][:, -lines:]
        store = pltpu.make_async_copy(sums, out, sems.at[len(sources)])
        store.start()
        store.wait()
        return
    result = None
    for i in range(blocks):
        v = totals[i] + before[0][:, i * lines : (i + 1) * lines]
        vh = v.astype(BF)
        vl = (v - vh.astype(F32)).astype(BF)
        both = jnp.concatenate([vh, vl], axis=1)
        a = jnp.dot(basis[2 * i][...], both, preferred_element_type=F32)
        b = jnp.dot(basis[2 * i + 1][...], vh, preferred_element_type=F32)
        part = a[:, :lines] + a[:, lines:] + b
        result = part if result is None else result + part
    out[...] = (result * scale).T


def plain_kernel(rt, *refs):
    packs, (out, w, oh, lev, sems, sums, held) = refs[:-7], refs[-7:]
    load = pltpu.make_async_copy(rt, held, sems.at[0])
    load.start()
    prepare(packs, w, oh, lev)
    load.wait()
    for s0 in range(0, rt.shape[0], CHUNK):
        sums[s0 : s0 + CHUNK, :] = chunk_values(
            held[s0 : s0 + CHUNK, :], w, oh, lev, packs[0].shape[1]
        )
    store = pltpu.make_async_copy(sums, out, sems.at[1])
    store.start()
    store.wait()


VSPEC = pl.BlockSpec(memory_space=pltpu.VMEM)
SSPEC = pl.BlockSpec(memory_space=pltpu.SMEM)
HSPEC = pl.BlockSpec(memory_space=pltpu.HBM)


def like(arrays):
    return [pltpu.VMEM(a.shape, a.dtype) for a in arrays]


def point_scratch(double, lines, points):
    return [
        pltpu.VMEM((double, points), BF),
        pltpu.VMEM((lines, points), BF),
        pltpu.VMEM((1, points), F32),
    ]


def values_of(rts, packs, lines, before=(), basis=(), scale=None):
    own, double = rts[0].shape
    points = packs[0].shape[1]
    pairs = own * points * len(rts) * len(packs)
    held = [*rts, *before, *basis]
    scratch = point_scratch(double, lines, points * len(packs))
    scratch.append(pltpu.SemaphoreType.DMA((len(held) + 1,)))
    kernel = functools.partial(value_kernel, len(rts), len(packs), len(before), scale)
    out = HSPEC
    if scale:
        shape = jax.ShapeDtypeStruct((lines, basis[0].shape[0]), F32)
        out = VSPEC
    else:
        shape = jax.ShapeDtypeStruct((own, lines * len(rts)), F32)
        scratch += like([shape])
    if not before:
        kernel = plain_kernel
    return pl.pallas_call(
        kernel,
        in_specs=[HSPEC] * len(rts)
        + [VSPEC] * len(packs)
        + [HSPEC] * (len(before) + len(basis)),
        out_specs=out,
        out_shape=shape,
        scratch_shapes=scratch + like(held),
        compiler_params=params(),
        cost_estimate=pl.CostEstimate(
            flops=1700 * pairs, bytes_accessed=2**20, transcendentals=pairs
        ),
    )(*rts, *packs, *before, *basis)


def picks_of(exps):
    count = exps.shape[1]
    e = exps[...].astype(F32)
    row = lax.broadcasted_iota(jnp.int32, (count, count), 0)
    col = lax.broadcasted_iota(jnp.int32, (count, count), 1)
    upto = (row <= col).astype(BF)
    cum = jnp.dot(e.astype(BF), upto, preferred_element_type=F32)
    before = cum - e
    picks = [
        jnp.where((cum > t + 0.5) & (before < t + 0.5), 1.0, 0.0).astype(BF) for t in range(3)
    ]
    return [jnp.concatenate([p, p], axis=1) for p in picks]


def basis_kernel(exps, scens, high, low, rt):
    factors = rt.shape[1] // 2
    r = scens[:factors, :].astype(F32).T.astype(BF)
    rt[:, :factors] = r
    rt[:, factors:] = r
    picks = picks_of(exps)
    for c in range(0, scens.shape[1], CHUNK):
        part = scens[factors:, c : c + CHUNK]
        x = [jnp.dot(p, part, preferred_element_type=F32) for p in picks]
        b = x[0] * x[1] * x[2]
        h = b.astype(BF)
        high[:, c : c + CHUNK] = h
        low[:, c : c + CHUNK] = (b - h.astype(F32)).astype(BF)


def first_kernel(exps, scens, p0, p1, *refs):
    outs, (w, oh, lev, sems, packs, *held) = refs[:4], refs[4:]
    loads = [pltpu.make_async_copy(p, packs.at[i], sems.at[4 + i]) for i, p in enumerate((p0, p1))]
    for load in loads:
        load.start()
    stores = [pltpu.make_async_copy(a, b, sems.at[i]) for i, (a, b) in enumerate(zip(held, outs))]
    basis_kernel(exps, scens, *held[:3])
    for store in stores[:3]:
        store.start()
    for load in loads:
        load.wait()
    prepare([packs.at[0], packs.at[1]], w, oh, lev)
    points = packs.shape[2]
    for s0 in range(0, held[2].shape[0], CHUNK):
        held[3][s0 : s0 + CHUNK, :] = chunk_values(
            held[2][s0 : s0 + CHUNK, :], w, oh, lev, points
        )
    stores[3].start()
    for store in stores:
        store.wait()


def gram_kernel(start, exps, scens, earlier, *refs):
    outs, keep, send, (sems, first, *held) = refs[:3], refs[3], refs[4], refs[5:]
    load = pltpu.make_async_copy(earlier, first, sems.at[3])
    load.start()
    stores = [pltpu.make_async_copy(a, b, sems.at[i]) for i, (a, b) in enumerate(zip(held, outs))]
    high = held[0]
    basis_kernel(exps, scens, *held)
    for store in stores:
        store.start()
    load.wait()
    rows = keep.shape[0]
    for i, out in enumerate((keep, send)):
        r0 = pl.multiple_of(start[i] * rows, rows)
        total = None
        for b in (first, high):
            part = lax.dot_general(
                b[pl.ds(r0, rows), :], b[...], (((1,), (1,)), ((), ())), preferred_element_type=F32
            )
            total = part if total is None else total + part
        out[...] = total
    for store in stores:
        store.wait()


def basis_of(exponents, scens, near=(), lines=0, start=None, first=None):
    terms, count = exponents.shape
    factors, own = scens.shape[0] - 2 * count, scens.shape[1]
    shapes = [jax.ShapeDtypeStruct((terms, own), BF)] * 2
    shapes.append(jax.ShapeDtypeStruct((own, 2 * factors), BF))
    cost = pl.CostEstimate(flops=3 * 10**9, bytes_accessed=3 * 2**20, transcendentals=0)
    if start is None:
        points = near[0].shape[1]
        shapes.append(jax.ShapeDtypeStruct((own, lines), F32))
        return pl.pallas_call(
            first_kernel,
            in_specs=[VSPEC] * 2 + [HSPEC] * 2,
            out_specs=[HSPEC] * 4,
            out_shape=shapes,
            scratch_shapes=point_scratch(2 * factors, lines, 2 * points)
            + [pltpu.SemaphoreType.DMA((6,)), pltpu.VMEM((2, *near[0].shape), BF)]
            + like(shapes),
            compiler_params=params(),
            cost_estimate=cost,
        )(exponents, scens, *near)
    scratch = [pltpu.SemaphoreType.DMA((4,)), *like([first]), *like(shapes)]
    shapes += [jax.ShapeDtypeStruct((terms // 4, terms), F32)] * 2
    return pl.pallas_call(
        gram_kernel,
        in_specs=[SSPEC, VSPEC, VSPEC, HSPEC],
        out_specs=[HSPEC] * 3 + [VSPEC] * 2,
        out_shape=shapes,
        scratch_shapes=scratch,
        compiler_params=params(),
        cost_estimate=cost,
    )(start, exponents, scens, first)


def place_kernel(blocks, *refs):
    order, pieces, out = refs[0], refs[1:-1], refs[-1]
    rows = out.shape[0] // blocks
    k = 0
    for piece in pieces:
        for i in range(piece.shape[0] // rows):
            at = pl.multiple_of(order[k] * rows, rows)
            out[pl.ds(at, rows), :] = piece[i * rows : (i + 1) * rows, :]
            k += 1


def placed(blocks, order, pieces, terms):
    return pl.pallas_call(
        functools.partial(place_kernel, blocks),
        in_specs=[pl.BlockSpec(memory_space=pltpu.SMEM)]
        + [pl.BlockSpec(memory_space=pltpu.VMEM)] * len(pieces),
        out_shape=jax.ShapeDtypeStruct((terms, terms), F32),
        compiler_params=params(),
        cost_estimate=pl.CostEstimate(
            flops=2**20, bytes_accessed=2 * 2**20, transcendentals=0
        ),
    )(order, *pieces)


def after(x, done):
    return lax.optimization_barrier((x, done))[0]


def local(n, returns, exposures, guarantees, guar_type, line_ids, drivers, exponents):
    lines = LINES
    scen_total = returns.shape[1] * n
    all_points = exposures.shape[0] * n
    terms = exponents.shape[0]
    me = lax.axis_index("scen").astype(jnp.int32)
    core, side = me & 1, (me >> 1) & 1

    def swap(x, mask):
        return lax.ppermute(x, "scen", [(i, i ^ mask) for i in range(n)])

    far = list(range(4, n, 4))
    deep = [4 << i for i in range((n // 4).bit_length() - 1)]
    scale = 1.0 / (math.sqrt(all_points / lines) * scen_total)
    pack, scens0 = packs_of(exposures, guarantees, guar_type, line_ids, returns, drivers)

    near = (pack, swap(pack, 1))
    scens1 = swap(scens0, 2)
    packs = {m: swap(pack, m) for m in far}

    high0, low0, rt0, v = basis_of(exponents, scens0, near, lines)
    before = [v]

    base = side * 2 + core
    start = jnp.stack([base, base ^ 1])
    high1, low1, rt1, keep, send = basis_of(
        exponents, after(scens1, v), start=start, first=high0
    )
    more = swap(send, 1)
    relays = {4: swap(after(packs[4], send), 1)}
    v = values_of([rt1], near, lines)
    before.append(v)
    keep, more = after((keep, more), v)
    gram = (keep + more) * (1.0 / scen_total)

    for m in far[1:]:
        relays[m] = swap(after(packs[m], v), 1)
    calls = [[packs[m], relays[m]] for m in far[:-1]] + [[packs[far[-1]]], [relays[far[-1]]]]
    rts = [rt0, rt1]
    steps, other = list(deep), None
    for i, call in enumerate(calls):
        last = i == len(calls) - 1
        if other is not None and (steps or last):
            gram = mine.astype(F32) + after(other, v).astype(F32)
            other = None
        if steps:
            mine = gram.astype(HALF)
            other = swap(mine, steps.pop(0))
        call = after(call, gram)
        if not last:
            v = values_of(rts, call, lines, before)
            before = [v]
    rhs = values_of(rts, call, lines, before, (high0, low0, high1, low1), scale)

    rhs = rhs + swap(rhs, 1)
    for m in [2] + deep:
        mine = rhs.astype(HALF)
        other = swap(mine, m)
        if m == deep[-1]:
            c = swap(jnp.concatenate([a, b], axis=0), 1)
            order = jnp.stack([base ^ k for k in (0, 2, 1, 3)])
            gram = placed(4, order, [x.astype(F32) for x in (a, b, c)], terms)
            other = after(other, gram)
        rhs = mine.astype(F32) + other.astype(F32)
        if m == 2:
            a = after(gram, rhs).astype(HALF)
            b = swap(a, 2)
    return (gram, rhs.T)


def solution(mesh):
    spots = (
        P(None, ("grp", "scen")),
        P(("grp", "scen"), None),
        P(("grp", "scen")),
        P(("grp", "scen")),
        P(("grp", "scen")),
        P(None, ("grp", "scen")),
        P(),
    )
    return jax.shard_map(
        functools.partial(local, mesh.shape["scen"]),
        mesh=mesh,
        in_specs=spots,
        out_specs=(P("grp", None), P("grp", None)),
        check_vma=False,
    )
```

```python
import functools
import math

import jax
import jax.numpy as jnp
from jax import lax
from jax.experimental import pallas as pl
from jax.experimental.pallas import tpu as pltpu
from jax.sharding import PartitionSpec as P

LINES = 64
TAIL = 16
CHUNK = 512
LOG2E = 1.4426950408889634
BF = jnp.bfloat16
F32 = jnp.float32
HALF = jnp.float16
VMEM = 24 * 2**20


def params(limit=VMEM):
    return pltpu.CompilerParams(vmem_limit_bytes=limit)


def parts_of(x, count):
    parts = []
    for _ in range(count):
        parts.append(x.astype(BF).astype(F32))
        x = x - parts[-1]
    return parts


def pack_kernel(*refs):
    points, scens = refs[6:8]
    held, sems = refs[8:14], refs[14]
    loads = [pltpu.make_async_copy(refs[i], held[i], sems.at[i]) for i in range(6)]
    for load in loads:
        load.start()
    for load in loads:
        load.wait()
    exposures, guarantees, kinds, lines, returns, drivers = held
    factors = exposures.shape[0]
    points[:factors, :] = exposures[...]
    level = guarantees[...] * (1.0 + 0.15 * kinds[...].astype(F32))
    rows = [*parts_of(level, 3), lines[...].astype(F32)]
    rows.append(jnp.zeros((TAIL - 4, level.shape[1]), F32))
    points[factors:, :] = jnp.concatenate(rows, axis=0).astype(BF)
    scens[:factors, :] = returns[...]
    scens[factors:, :] = jnp.concatenate(parts_of(drivers[...], 2), axis=0).astype(BF)


def packs_of(exposures, guarantees, kinds, lines, returns, drivers):
    points, factors = exposures.shape
    row = (1, points)
    args = (
        exposures.T,
        guarantees.reshape(row),
        kinds.reshape(row),
        lines.reshape(row),
        returns,
        drivers,
    )
    return pl.pallas_call(
        pack_kernel,
        in_specs=[pl.BlockSpec(memory_space=pltpu.HBM)] * len(args),
        out_shape=[
            jax.ShapeDtypeStruct((factors + TAIL, points), BF),
            jax.ShapeDtypeStruct((factors + 2 * drivers.shape[0], returns.shape[1]), BF),
        ],
        scratch_shapes=[pltpu.VMEM(a.shape, a.dtype) for a in args]
        + [pltpu.SemaphoreType.DMA((len(args),))],
        compiler_params=params(58 * 2**20),
        cost_estimate=pl.CostEstimate(flops=2**20, bytes_accessed=2**20, transcendentals=0),
    )(*args)


def prepare(packs, w, oh, lev):
    factors = w.shape[0] // 2
    points = packs[0].shape[1]
    for i, pack in enumerate(packs):
        at = slice(i * points, (i + 1) * points)
        e = pack[:factors, :].astype(F32) * LOG2E
        high = e.astype(BF)
        w[:factors, at] = high
        w[factors:, at] = (e - high.astype(F32)).astype(BF)
        tail = pack[factors:, :].astype(F32)
        lev[:, at] = tail[0:1] + tail[1:2] + tail[2:3]
        label = lax.broadcasted_iota(jnp.int32, (oh.shape[0], points), 0).astype(F32)
        oh[:, at] = (label == tail[3:4]).astype(BF)


def chunk_values(r, w, oh, lev, step):
    total = None
    for j in range(0, w.shape[1], step):
        at = slice(j, j + step)
        power = jnp.dot(r, w[:, at], preferred_element_type=F32)
        payoff = jnp.maximum(lev[:, at] - jnp.exp2(power), 0.0).astype(BF)
        part = lax.dot_general(
            payoff, oh[:, at], (((1,), (1,)), ((), ())), preferred_element_type=F32
        )
        total = part if total is None else total + part
    return total


def value_kernel(blocks, count, rows, earlier, scale, *refs):
    rts, refs = refs[:blocks], refs[blocks:]
    height = rts[0].shape[1] // 2 + TAIL
    packs = [refs[i].at[r : r + height] for i, r in rows]
    refs = refs[count:]
    before, refs = refs[:earlier], refs[earlier:]
    sources = [*rts, *before]
    if scale:
        basis, refs = refs[: 2 * blocks], refs[2 * blocks :]
        out, w, oh, lev, sems, *held = refs
        sources += basis
    else:
        out, w, oh, lev, sems, sums, *held = refs
    loads = [pltpu.make_async_copy(a, b, sems.at[i]) for i, (a, b) in enumerate(zip(sources, held))]
    for load in loads:
        load.start()
    own = rts[0].shape[0]
    points = packs[0].shape[1]
    lines = oh.shape[0]
    prepare(packs, w, oh, lev)
    for load in loads[:blocks]:
        load.wait()
    totals = [
        [
            chunk_values(held[i][s0 : s0 + CHUNK, :], w, oh, lev, points)
            for s0 in range(0, own, CHUNK)
        ]
        for i in range(blocks)
    ]
    for load in loads[blocks:]:
        load.wait()
    before, basis = held[blocks : blocks + earlier], held[blocks + earlier :]
    totals = [jnp.concatenate(t, axis=0) for t in totals]
    if not scale:
        sums[:, :lines] = totals[0] + before[0][:, :lines]
        sums[:, lines:] = totals[1] + before[-1][:, -lines:]
        store = pltpu.make_async_copy(sums, out, sems.at[len(sources)])
        store.start()
        store.wait()
        return
    result = None
    for i in range(blocks):
        v = totals[i] + before[0][:, i * lines : (i + 1) * lines]
        vh = v.astype(BF)
        vl = (v - vh.astype(F32)).astype(BF)
        both = jnp.concatenate([vh, vl], axis=1)
        a = jnp.dot(basis[2 * i][...], both, preferred_element_type=F32)
        b = jnp.dot(basis[2 * i + 1][...], vh, preferred_element_type=F32)
        part = a[:, :lines] + a[:, lines:] + b
        result = part if result is None else result + part
    out[...] = (result * scale).T


def plain_kernel(rt, *refs):
    packs, (out, w, oh, lev, sems, sums, held) = refs[:-7], refs[-7:]
    load = pltpu.make_async_copy(rt, held, sems.at[0])
    load.start()
    prepare(packs, w, oh, lev)
    load.wait()
    for s0 in range(0, rt.shape[0], CHUNK):
        sums[s0 : s0 + CHUNK, :] = chunk_values(
            held[s0 : s0 + CHUNK, :], w, oh, lev, packs[0].shape[1]
        )
    store = pltpu.make_async_copy(sums, out, sems.at[1])
    store.start()
    store.wait()


VSPEC = pl.BlockSpec(memory_space=pltpu.VMEM)
SSPEC = pl.BlockSpec(memory_space=pltpu.SMEM)
HSPEC = pl.BlockSpec(memory_space=pltpu.HBM)


def like(arrays):
    return [pltpu.VMEM(a.shape, a.dtype) for a in arrays]


def point_scratch(double, lines, points):
    return [
        pltpu.VMEM((double, points), BF),
        pltpu.VMEM((lines, points), BF),
        pltpu.VMEM((1, points), F32),
    ]


def values_of(rts, packs, lines, before=(), basis=(), scale=None, rows=None):
    own, double = rts[0].shape
    points = packs[0].shape[1]
    rows = rows or [(i, 0) for i in range(len(packs))]
    pairs = own * points * len(rts) * len(rows)
    held = [*rts, *before, *basis]
    scratch = point_scratch(double, lines, points * len(rows))
    scratch.append(pltpu.SemaphoreType.DMA((len(held) + 1,)))
    kernel = functools.partial(value_kernel, len(rts), len(packs), rows, len(before), scale)
    out = HSPEC
    if scale:
        shape = jax.ShapeDtypeStruct((lines, basis[0].shape[0]), F32)
        out = VSPEC
    else:
        shape = jax.ShapeDtypeStruct((own, lines * len(rts)), F32)
        scratch += like([shape])
    if not before:
        kernel = plain_kernel
    return pl.pallas_call(
        kernel,
        in_specs=[HSPEC] * len(rts)
        + [VSPEC] * len(packs)
        + [HSPEC] * (len(before) + len(basis)),
        out_specs=out,
        out_shape=shape,
        scratch_shapes=scratch + like(held),
        compiler_params=params(),
        cost_estimate=pl.CostEstimate(
            flops=1700 * pairs, bytes_accessed=2**20, transcendentals=pairs
        ),
    )(*rts, *packs, *before, *basis)


def picks_of(exps):
    count = exps.shape[1]
    e = exps[...].astype(F32)
    row = lax.broadcasted_iota(jnp.int32, (count, count), 0)
    col = lax.broadcasted_iota(jnp.int32, (count, count), 1)
    upto = (row <= col).astype(BF)
    cum = jnp.dot(e.astype(BF), upto, preferred_element_type=F32)
    before = cum - e
    picks = [
        jnp.where((cum > t + 0.5) & (before < t + 0.5), 1.0, 0.0).astype(BF) for t in range(3)
    ]
    return [jnp.concatenate([p, p], axis=1) for p in picks]


def basis_kernel(exps, scens, high, low, rt):
    factors = rt.shape[1] // 2
    r = scens[:factors, :].astype(F32).T.astype(BF)
    rt[:, :factors] = r
    rt[:, factors:] = r
    picks = picks_of(exps)
    for c in range(0, scens.shape[1], CHUNK):
        part = scens[factors:, c : c + CHUNK]
        x = [jnp.dot(p, part, preferred_element_type=F32) for p in picks]
        b = x[0] * x[1] * x[2]
        h = b.astype(BF)
        high[:, c : c + CHUNK] = h
        low[:, c : c + CHUNK] = (b - h.astype(F32)).astype(BF)


def first_kernel(exps, scens, p0, p1, *refs):
    outs, (w, oh, lev, sems, packs, *held) = refs[:4], refs[4:]
    loads = [pltpu.make_async_copy(p, packs.at[i], sems.at[4 + i]) for i, p in enumerate((p0, p1))]
    for load in loads:
        load.start()
    stores = [pltpu.make_async_copy(a, b, sems.at[i]) for i, (a, b) in enumerate(zip(held, outs))]
    basis_kernel(exps, scens, *held[:3])
    for store in stores[:3]:
        store.start()
    for load in loads:
        load.wait()
    prepare([packs.at[0], packs.at[1]], w, oh, lev)
    points = packs.shape[2]
    for s0 in range(0, held[2].shape[0], CHUNK):
        held[3][s0 : s0 + CHUNK, :] = chunk_values(
            held[2][s0 : s0 + CHUNK, :], w, oh, lev, points
        )
    stores[3].start()
    for store in stores:
        store.wait()


def gram_kernel(start, exps, scens, earlier, *refs):
    outs, keep, send, (sems, first, *held) = refs[:3], refs[3], refs[4], refs[5:]
    load = pltpu.make_async_copy(earlier, first, sems.at[3])
    load.start()
    stores = [pltpu.make_async_copy(a, b, sems.at[i]) for i, (a, b) in enumerate(zip(held, outs))]
    high = held[0]
    basis_kernel(exps, scens, *held)
    for store in stores:
        store.start()
    load.wait()
    rows = keep.shape[0]
    for i, out in enumerate((keep, send)):
        r0 = pl.multiple_of(start[i] * rows, rows)
        total = None
        for b in (first, high):
            part = lax.dot_general(
                b[pl.ds(r0, rows), :], b[...], (((1,), (1,)), ((), ())), preferred_element_type=F32
            )
            total = part if total is None else total + part
        out[...] = total
    for store in stores:
        store.wait()


def basis_of(exponents, scens, near=(), lines=0, start=None, first=None):
    terms, count = exponents.shape
    factors, own = scens.shape[0] - 2 * count, scens.shape[1]
    shapes = [jax.ShapeDtypeStruct((terms, own), BF)] * 2
    shapes.append(jax.ShapeDtypeStruct((own, 2 * factors), BF))
    cost = pl.CostEstimate(flops=3 * 10**9, bytes_accessed=3 * 2**20, transcendentals=0)
    if start is None:
        points = near[0].shape[1]
        shapes.append(jax.ShapeDtypeStruct((own, lines), F32))
        return pl.pallas_call(
            first_kernel,
            in_specs=[VSPEC] * 2 + [HSPEC] * 2,
            out_specs=[HSPEC] * 4,
            out_shape=shapes,
            scratch_shapes=point_scratch(2 * factors, lines, 2 * points)
            + [pltpu.SemaphoreType.DMA((6,)), pltpu.VMEM((2, *near[0].shape), BF)]
            + like(shapes),
            compiler_params=params(),
            cost_estimate=cost,
        )(exponents, scens, *near)
    scratch = [pltpu.SemaphoreType.DMA((4,)), *like([first]), *like(shapes)]
    shapes += [jax.ShapeDtypeStruct((terms // 4, terms), F32)] * 2
    return pl.pallas_call(
        gram_kernel,
        in_specs=[SSPEC, VSPEC, VSPEC, HSPEC],
        out_specs=[HSPEC] * 3 + [VSPEC] * 2,
        out_shape=shapes,
        scratch_shapes=scratch,
        compiler_params=params(),
        cost_estimate=cost,
    )(start, exponents, scens, first)


def place_kernel(blocks, *refs):
    order, pieces, out = refs[0], refs[1:-1], refs[-1]
    rows = out.shape[0] // blocks
    k = 0
    for piece in pieces:
        for i in range(piece.shape[0] // rows):
            at = pl.multiple_of(order[k] * rows, rows)
            out[pl.ds(at, rows), :] = piece[i * rows : (i + 1) * rows, :]
            k += 1


def placed(blocks, order, pieces, terms):
    return pl.pallas_call(
        functools.partial(place_kernel, blocks),
        in_specs=[pl.BlockSpec(memory_space=pltpu.SMEM)]
        + [pl.BlockSpec(memory_space=pltpu.VMEM)] * len(pieces),
        out_shape=jax.ShapeDtypeStruct((terms, terms), F32),
        compiler_params=params(),
        cost_estimate=pl.CostEstimate(
            flops=2**20, bytes_accessed=2 * 2**20, transcendentals=0
        ),
    )(order, *pieces)


def after(x, done):
    return lax.optimization_barrier((x, done))[0]


def local(n, returns, exposures, guarantees, guar_type, line_ids, drivers, exponents):
    lines = LINES
    scen_total = returns.shape[1] * n
    all_points = exposures.shape[0] * n
    terms = exponents.shape[0]
    me = lax.axis_index("scen").astype(jnp.int32)
    core, side = me & 1, (me >> 1) & 1

    def swap(x, mask):
        return lax.ppermute(x, "scen", [(i, i ^ mask) for i in range(n)])

    deep = [4 << i for i in range((n // 4).bit_length() - 1)]
    scale = 1.0 / (math.sqrt(all_points / lines) * scen_total)
    pack, scens0 = packs_of(exposures, guarantees, guar_type, line_ids, returns, drivers)

    near = (pack, swap(pack, 1))
    scens1 = swap(scens0, 2)
    packs = {m: swap(pack, m) for m in deep}

    high0, low0, rt0, v = basis_of(exponents, scens0, near, lines)
    before = [v]
    packs[4] = after(packs[4], v)
    relay = swap(packs[4], 1)
    far = range(8, n, 4)
    for m in far:
        if m not in packs:
            top = max(h for h in deep if h <= m)
            packs[m] = swap(packs[m ^ top], top)

    base = side * 2 + core
    start = jnp.stack([base, base ^ 1])
    high1, low1, rt1, keep, send = basis_of(
        exponents, after(scens1, v), start=start, first=high0
    )
    more = swap(send, 1)
    v = values_of([rt1], near, lines)
    before.append(v)
    keep, more = after((keep, more), v)
    gram = (keep + more) * (1.0 / scen_total)

    pairs = [(m, m + 4) for m in range(8, n, 8)]
    calls = [(4,), *pairs, *[(m ^ 1, k ^ 1) for m, k in pairs[:-1]]]
    calls += [(m ^ 1,) for m in pairs[-1]]
    rts = [rt0, rt1]
    steps, other = list(deep), None
    for i, call in enumerate(calls):
        last = i == len(calls) - 1
        if other is not None and (steps or last):
            gram = mine.astype(F32) + after(other, v).astype(F32)
            other = None
        if i == 1:
            for m in far:
                packs[m ^ 1] = swap(after(packs[m], v), 1)
        if steps:
            mine = gram.astype(HALF)
            other = swap(mine, steps.pop(0))
        call = [packs[m] for m in call] + ([relay] if i == 0 else [])
        call = after(call, gram)
        if not last:
            v = values_of(rts, call, lines, before)
            before = [v]
    basis = (high0, low0, high1, low1)
    rhs = values_of(rts, call, lines, before, basis, scale)

    rhs = rhs + swap(rhs, 1)
    for m in [2] + deep:
        mine = rhs.astype(HALF)
        other = swap(mine, m)
        if m == deep[-1]:
            c = swap(jnp.concatenate([a, b], axis=0), 1)
            order = jnp.stack([base ^ k for k in (0, 2, 1, 3)])
            gram = placed(4, order, [x.astype(F32) for x in (a, b, c)], terms)
            other = after(other, gram)
        rhs = mine.astype(F32) + other.astype(F32)
        if m == 2:
            a = after(gram, rhs).astype(HALF)
            b = swap(a, 2)
    return (gram, rhs.T)


def solution(mesh):
    spots = (
        P(None, ("grp", "scen")),
        P(("grp", "scen"), None),
        P(("grp", "scen")),
        P(("grp", "scen")),
        P(("grp", "scen")),
        P(None, ("grp", "scen")),
        P(),
    )
    return jax.shard_map(
        functools.partial(local, mesh.shape["scen"]),
        mesh=mesh,
        in_specs=spots,
        out_specs=(P("grp", None), P("grp", None)),
        check_vma=False,
    )
```

```python
import functools
import math

import jax
import jax.numpy as jnp
from jax import lax
from jax.experimental import pallas as pl
from jax.experimental.pallas import tpu as pltpu
from jax.sharding import PartitionSpec as P

LINES = 64
TAIL = 16
CHUNK = 512
ROWS = 256
TILE = 2**18
LOG2E = 1.4426950408889634
BF = jnp.bfloat16
F32 = jnp.float32
HALF = jnp.float16
VMEM = 24 * 2**20


def params(limit=VMEM):
    return pltpu.CompilerParams(vmem_limit_bytes=limit)


def parts_of(x, count):
    parts = []
    for _ in range(count):
        parts.append(x.astype(BF).astype(F32))
        x = x - parts[-1]
    return parts


def pack_kernel(*refs):
    points, scens = refs[6:8]
    held, sems = refs[8:14], refs[14]
    loads = [pltpu.make_async_copy(refs[i], held[i], sems.at[i]) for i in range(6)]
    for load in loads:
        load.start()
    for load in loads:
        load.wait()
    exposures, guarantees, kinds, lines, returns, drivers = held
    factors = exposures.shape[0]
    points[:factors, :] = exposures[...]
    level = guarantees[...] * (1.0 + 0.15 * kinds[...].astype(F32))
    rows = [*parts_of(level, 3), lines[...].astype(F32)]
    rows.append(jnp.zeros((TAIL - 4, level.shape[1]), F32))
    points[factors:, :] = jnp.concatenate(rows, axis=0).astype(BF)
    scens[:factors, :] = returns[...]
    scens[factors:, :] = jnp.concatenate(parts_of(drivers[...], 2), axis=0).astype(BF)


def packs_of(exposures, guarantees, kinds, lines, returns, drivers):
    points, factors = exposures.shape
    row = (1, points)
    args = (
        exposures.T,
        guarantees.reshape(row),
        kinds.reshape(row),
        lines.reshape(row),
        returns,
        drivers,
    )
    return pl.pallas_call(
        pack_kernel,
        in_specs=[pl.BlockSpec(memory_space=pltpu.HBM)] * len(args),
        out_shape=[
            jax.ShapeDtypeStruct((factors + TAIL, points), BF),
            jax.ShapeDtypeStruct((factors + 2 * drivers.shape[0], returns.shape[1]), BF),
        ],
        scratch_shapes=[pltpu.VMEM(a.shape, a.dtype) for a in args]
        + [pltpu.SemaphoreType.DMA((len(args),))],
        compiler_params=params(58 * 2**20),
        cost_estimate=pl.CostEstimate(flops=2**20, bytes_accessed=2**20, transcendentals=0),
    )(*args)


def prepare(packs, w, oh, lev):
    factors = w.shape[0] // 2
    points = packs[0].shape[1]
    for i, pack in enumerate(packs):
        at = slice(i * points, (i + 1) * points)
        e = pack[:factors, :].astype(F32) * LOG2E
        high = e.astype(BF)
        w[:factors, at] = high
        w[factors:, at] = (e - high.astype(F32)).astype(BF)
        tail = pack[factors:, :].astype(F32)
        lev[:, at] = tail[0:1] + tail[1:2] + tail[2:3]
        label = lax.broadcasted_iota(jnp.int32, (oh.shape[0], points), 0).astype(F32)
        oh[:, at] = (label == tail[3:4]).astype(BF)


def chunk_values(r, w, oh, lev):
    power = jnp.dot(r, w[...], preferred_element_type=F32)
    payoff = jnp.maximum(lev[...] - jnp.exp2(power), 0.0).astype(BF)
    return lax.dot_general(
        payoff, oh[...], (((1,), (1,)), ((), ())), preferred_element_type=F32
    )


def value_kernel(blocks, count, rows, earlier, scale, *refs):
    rts, refs = refs[:blocks], refs[blocks:]
    height = rts[0].shape[1] // 2 + TAIL
    packs = [refs[i].at[r : r + height] for i, r in rows]
    refs = refs[count:]
    before, refs = refs[:earlier], refs[earlier:]
    sources = list(rts)
    if scale:
        basis, refs = refs[: 2 * blocks], refs[2 * blocks :]
        out, w, oh, lev, sems, *held = refs
        sources += basis
    else:
        out, w, oh, lev, sems, *held = refs
    loads = [pltpu.make_async_copy(a, b, sems.at[i]) for i, (a, b) in enumerate(zip(sources, held))]
    for load in loads:
        load.start()
    own = rts[0].shape[0]
    lines = oh.shape[0]
    prepare(packs, w, oh, lev)
    for load in loads[:blocks]:
        load.wait()
    totals = [
        [
            chunk_values(held[i][s0 : s0 + ROWS, :], w, oh, lev)
            for s0 in range(0, own, ROWS)
        ]
        for i in range(blocks)
    ]
    for load in loads[blocks:]:
        load.wait()
    basis = held[blocks:]
    totals = [jnp.concatenate(t, axis=0) for t in totals]
    if not scale:
        out[:, :lines] = totals[0] + before[0][:, :lines]
        out[:, lines:] = totals[1] + before[-1][:, -lines:]
        return
    result = None
    for i in range(blocks):
        v = totals[i] + before[0][:, i * lines : (i + 1) * lines]
        vh = v.astype(BF)
        vl = (v - vh.astype(F32)).astype(BF)
        both = jnp.concatenate([vh, vl], axis=1)
        a = jnp.dot(basis[2 * i][...], both, preferred_element_type=F32)
        b = jnp.dot(basis[2 * i + 1][...], vh, preferred_element_type=F32)
        part = a[:, :lines] + a[:, lines:] + b
        result = part if result is None else result + part
    out[...] = (result * scale).T


def plain_kernel(rt, *refs):
    packs, (out, w, oh, lev, sems, held) = refs[:-6], refs[-6:]
    load = pltpu.make_async_copy(rt, held, sems.at[0])
    load.start()
    prepare(packs, w, oh, lev)
    load.wait()
    rows = TILE // w.shape[1]
    for s0 in range(0, rt.shape[0], rows):
        out[s0 : s0 + rows, :] = chunk_values(held[s0 : s0 + rows, :], w, oh, lev)


VSPEC = pl.BlockSpec(memory_space=pltpu.VMEM)
SSPEC = pl.BlockSpec(memory_space=pltpu.SMEM)
HSPEC = pl.BlockSpec(memory_space=pltpu.HBM)


def like(arrays):
    return [pltpu.VMEM(a.shape, a.dtype) for a in arrays]


def point_scratch(double, lines, points):
    return [
        pltpu.VMEM((double, points), BF),
        pltpu.VMEM((lines, points), BF),
        pltpu.VMEM((1, points), F32),
    ]


def values_of(rts, packs, lines, before=(), basis=(), scale=None, rows=None):
    own, double = rts[0].shape
    points = packs[0].shape[1]
    rows = rows or [(i, 0) for i in range(len(packs))]
    pairs = own * points * len(rts) * len(rows)
    held = [*rts, *basis]
    scratch = point_scratch(double, lines, points * len(rows))
    scratch.append(pltpu.SemaphoreType.DMA((len(held),)))
    kernel = functools.partial(value_kernel, len(rts), len(packs), rows, len(before), scale)
    if scale:
        shape = jax.ShapeDtypeStruct((lines, basis[0].shape[0]), F32)
    else:
        shape = jax.ShapeDtypeStruct((own, lines * len(rts)), F32)
    if not before:
        kernel = plain_kernel
    return pl.pallas_call(
        kernel,
        in_specs=[HSPEC] * len(rts)
        + [VSPEC] * (len(packs) + len(before))
        + [HSPEC] * len(basis),
        out_specs=VSPEC,
        out_shape=shape,
        scratch_shapes=scratch + like(held),
        compiler_params=params(),
        cost_estimate=pl.CostEstimate(
            flops=1700 * pairs, bytes_accessed=2**20, transcendentals=pairs
        ),
    )(*rts, *packs, *before, *basis)


def picks_of(exps):
    count = exps.shape[1]
    e = exps[...].astype(F32)
    row = lax.broadcasted_iota(jnp.int32, (count, count), 0)
    col = lax.broadcasted_iota(jnp.int32, (count, count), 1)
    upto = (row <= col).astype(BF)
    cum = jnp.dot(e.astype(BF), upto, preferred_element_type=F32)
    before = cum - e
    picks = [
        jnp.where((cum > t + 0.5) & (before < t + 0.5), 1.0, 0.0).astype(BF) for t in range(3)
    ]
    return [jnp.concatenate([p, p], axis=1) for p in picks]


def basis_kernel(exps, scens, high, low, rt):
    factors = rt.shape[1] // 2
    r = scens[:factors, :].astype(F32).T.astype(BF)
    rt[:, :factors] = r
    rt[:, factors:] = r
    picks = picks_of(exps)
    for c in range(0, scens.shape[1], CHUNK):
        part = scens[factors:, c : c + CHUNK]
        x = [jnp.dot(p, part, preferred_element_type=F32) for p in picks]
        b = x[0] * x[1] * x[2]
        h = b.astype(BF)
        high[:, c : c + CHUNK] = h
        low[:, c : c + CHUNK] = (b - h.astype(F32)).astype(BF)


def first_kernel(exps, scens, p0, p1, *refs):
    outs, (w, oh, lev, sems, packs, *held) = refs[:4], refs[4:]
    loads = [pltpu.make_async_copy(p, packs.at[i], sems.at[4 + i]) for i, p in enumerate((p0, p1))]
    for load in loads:
        load.start()
    stores = [pltpu.make_async_copy(a, b, sems.at[i]) for i, (a, b) in enumerate(zip(held, outs))]
    basis_kernel(exps, scens, *held[:3])
    for store in stores[:3]:
        store.start()
    for load in loads:
        load.wait()
    prepare([packs.at[0], packs.at[1]], w, oh, lev)
    rows = TILE // w.shape[1]
    for s0 in range(0, held[2].shape[0], rows):
        held[3][s0 : s0 + rows, :] = chunk_values(held[2][s0 : s0 + rows, :], w, oh, lev)
    stores[3].start()
    for store in stores:
        store.wait()


def gram_kernel(start, exps, scens, earlier, *refs):
    outs, keep, send, (sems, first, *held) = refs[:3], refs[3], refs[4], refs[5:]
    load = pltpu.make_async_copy(earlier, first, sems.at[3])
    load.start()
    stores = [pltpu.make_async_copy(a, b, sems.at[i]) for i, (a, b) in enumerate(zip(held, outs))]
    high = held[0]
    basis_kernel(exps, scens, *held)
    for store in stores:
        store.start()
    load.wait()
    rows = keep.shape[0]
    for i, out in enumerate((keep, send)):
        r0 = pl.multiple_of(start[i] * rows, rows)
        total = None
        for b in (first, high):
            part = lax.dot_general(
                b[pl.ds(r0, rows), :], b[...], (((1,), (1,)), ((), ())), preferred_element_type=F32
            )
            total = part if total is None else total + part
        out[...] = total
    for store in stores:
        store.wait()


def basis_of(exponents, scens, near=(), lines=0, start=None, first=None):
    terms, count = exponents.shape
    factors, own = scens.shape[0] - 2 * count, scens.shape[1]
    shapes = [jax.ShapeDtypeStruct((terms, own), BF)] * 2
    shapes.append(jax.ShapeDtypeStruct((own, 2 * factors), BF))
    cost = pl.CostEstimate(flops=3 * 10**9, bytes_accessed=3 * 2**20, transcendentals=0)
    if start is None:
        points = near[0].shape[1]
        shapes.append(jax.ShapeDtypeStruct((own, lines), F32))
        return pl.pallas_call(
            first_kernel,
            in_specs=[VSPEC] * 2 + [HSPEC] * 2,
            out_specs=[HSPEC] * 4,
            out_shape=shapes,
            scratch_shapes=point_scratch(2 * factors, lines, 2 * points)
            + [pltpu.SemaphoreType.DMA((6,)), pltpu.VMEM((2, *near[0].shape), BF)]
            + like(shapes),
            compiler_params=params(),
            cost_estimate=cost,
        )(exponents, scens, *near)
    scratch = [pltpu.SemaphoreType.DMA((4,)), *like([first]), *like(shapes)]
    shapes += [jax.ShapeDtypeStruct((terms // 4, terms), F32)] * 2
    return pl.pallas_call(
        gram_kernel,
        in_specs=[SSPEC, VSPEC, VSPEC, HSPEC],
        out_specs=[HSPEC] * 3 + [VSPEC] * 2,
        out_shape=shapes,
        scratch_shapes=scratch,
        compiler_params=params(),
        cost_estimate=cost,
    )(start, exponents, scens, first)


def place_kernel(blocks, *refs):
    order, pieces, out = refs[0], refs[1:-1], refs[-1]
    rows = out.shape[0] // blocks
    k = 0
    for piece in pieces:
        for i in range(piece.shape[0] // rows):
            at = pl.multiple_of(order[k] * rows, rows)
            out[pl.ds(at, rows), :] = piece[i * rows : (i + 1) * rows, :]
            k += 1


def placed(blocks, order, pieces, terms):
    return pl.pallas_call(
        functools.partial(place_kernel, blocks),
        in_specs=[pl.BlockSpec(memory_space=pltpu.SMEM)]
        + [pl.BlockSpec(memory_space=pltpu.VMEM)] * len(pieces),
        out_shape=jax.ShapeDtypeStruct((terms, terms), F32),
        compiler_params=params(),
        cost_estimate=pl.CostEstimate(
            flops=2**20, bytes_accessed=2 * 2**20, transcendentals=0
        ),
    )(order, *pieces)


def after(x, done):
    return lax.optimization_barrier((x, done))[0]


def local(n, returns, exposures, guarantees, guar_type, line_ids, drivers, exponents):
    lines = LINES
    scen_total = returns.shape[1] * n
    all_points = exposures.shape[0] * n
    terms = exponents.shape[0]
    me = lax.axis_index("scen").astype(jnp.int32)
    core, side = me & 1, (me >> 1) & 1

    def swap(x, mask):
        return lax.ppermute(x, "scen", [(i, i ^ mask) for i in range(n)])

    deep = [4 << i for i in range((n // 4).bit_length() - 1)]
    scale = 1.0 / (math.sqrt(all_points / lines) * scen_total)
    pack, scens0 = packs_of(exposures, guarantees, guar_type, line_ids, returns, drivers)

    near = (pack, swap(pack, 1))
    scens1 = swap(scens0, 2)
    packs = {m: swap(pack, m) for m in deep}

    high0, low0, rt0, v = basis_of(exponents, scens0, near, lines)
    before = [v]
    packs[4] = after(packs[4], v)
    relay = swap(packs[4], 1)
    far = range(8, n, 4)
    for m in far:
        if m not in packs:
            top = max(h for h in deep if h <= m)
            packs[m] = swap(packs[m ^ top], top)

    base = side * 2 + core
    start = jnp.stack([base, base ^ 1])
    high1, low1, rt1, keep, send = basis_of(
        exponents, after(scens1, v), start=start, first=high0
    )
    more = swap(send, 1)
    v = values_of([rt1], near, lines)
    before.append(v)
    keep, more = after((keep, more), v)
    gram = (keep + more) * (1.0 / scen_total)

    pairs = [(m, m + 4) for m in range(8, n, 8)]
    calls = [(4,), *pairs, *[(m ^ 1, k ^ 1) for m, k in pairs[:-1]]]
    calls += [(m ^ 1,) for m in pairs[-1]]
    rts = [rt0, rt1]
    steps, other = list(deep), None
    for i, call in enumerate(calls):
        last = i == len(calls) - 1
        if other is not None and (steps or last):
            gram = mine.astype(F32) + after(other, v).astype(F32)
            other = None
        if i == 1:
            for m in far:
                packs[m ^ 1] = swap(after(packs[m], v), 1)
        if steps:
            mine = gram.astype(HALF)
            other = swap(mine, steps.pop(0))
        call = [packs[m] for m in call] + ([relay] if i == 0 else [])
        call = after(call, gram)
        if not last:
            v = values_of(rts, call, lines, before)
            before = [v]
    basis = (high0, low0, high1, low1)
    rhs = values_of(rts, call, lines, before, basis, scale)

    rhs = rhs + swap(rhs, 1)
    for m in [2] + deep:
        mine = rhs.astype(HALF)
        other = swap(mine, m)
        if m == deep[-1]:
            c = swap(jnp.concatenate([a, b], axis=0), 1)
            order = jnp.stack([base ^ k for k in (0, 2, 1, 3)])
            gram = placed(4, order, [x.astype(F32) for x in (a, b, c)], terms)
            other = after(other, gram)
        rhs = mine.astype(F32) + other.astype(F32)
        if m == 2:
            a = after(gram, rhs).astype(HALF)
            b = swap(a, 2)
    return (gram, rhs.T)


def solution(mesh):
    spots = (
        P(None, ("grp", "scen")),
        P(("grp", "scen"), None),
        P(("grp", "scen")),
        P(("grp", "scen")),
        P(("grp", "scen")),
        P(None, ("grp", "scen")),
        P(),
    )
    return jax.shard_map(
        functools.partial(local, mesh.shape["scen"]),
        mesh=mesh,
        in_specs=spots,
        out_specs=(P("grp", None), P("grp", None)),
        check_vma=False,
    )
```

```python
import functools
import math

import jax
import jax.numpy as jnp
from jax import lax
from jax.experimental import pallas as pl
from jax.experimental.pallas import tpu as pltpu
from jax.sharding import PartitionSpec as P

LINES = 64
TAIL = 16
CHUNK = 512
ROWS = 256
TILE = 2**18
LOG2E = 1.4426950408889634
BF = jnp.bfloat16
F32 = jnp.float32
HALF = jnp.float16
VMEM = 24 * 2**20


def params(limit=VMEM):
    return pltpu.CompilerParams(vmem_limit_bytes=limit)


def parts_of(x, count):
    parts = []
    for _ in range(count):
        parts.append(x.astype(BF).astype(F32))
        x = x - parts[-1]
    return parts


def pack_kernel(*refs):
    points, scens = refs[6:8]
    held, sems = refs[8:14], refs[14]
    loads = [pltpu.make_async_copy(refs[i], held[i], sems.at[i]) for i in range(6)]
    for load in loads:
        load.start()
    for load in loads:
        load.wait()
    exposures, guarantees, kinds, lines, returns, drivers = held
    factors = exposures.shape[0]
    points[:factors, :] = exposures[...]
    level = guarantees[...] * (1.0 + 0.15 * kinds[...].astype(F32))
    rows = [*parts_of(level, 3), lines[...].astype(F32)]
    rows.append(jnp.zeros((TAIL - 4, level.shape[1]), F32))
    points[factors:, :] = jnp.concatenate(rows, axis=0).astype(BF)
    scens[:factors, :] = returns[...]
    scens[factors:, :] = jnp.concatenate(parts_of(drivers[...], 2), axis=0).astype(BF)


def packs_of(exposures, guarantees, kinds, lines, returns, drivers):
    points, factors = exposures.shape
    row = (1, points)
    args = (
        exposures.T,
        guarantees.reshape(row),
        kinds.reshape(row),
        lines.reshape(row),
        returns,
        drivers,
    )
    return pl.pallas_call(
        pack_kernel,
        in_specs=[pl.BlockSpec(memory_space=pltpu.HBM)] * len(args),
        out_shape=[
            jax.ShapeDtypeStruct((factors + TAIL, points), BF),
            jax.ShapeDtypeStruct((factors + 2 * drivers.shape[0], returns.shape[1]), BF),
        ],
        scratch_shapes=[pltpu.VMEM(a.shape, a.dtype) for a in args]
        + [pltpu.SemaphoreType.DMA((len(args),))],
        compiler_params=params(58 * 2**20),
        cost_estimate=pl.CostEstimate(flops=2**20, bytes_accessed=2**20, transcendentals=0),
    )(*args)


def prepare(packs, w, oh, lev):
    factors = w.shape[0] // 2
    points = packs[0].shape[1]
    for i, pack in enumerate(packs):
        at = slice(i * points, (i + 1) * points)
        e = pack[:factors, :].astype(F32) * LOG2E
        high = e.astype(BF)
        w[:factors, at] = high
        w[factors:, at] = (e - high.astype(F32)).astype(BF)
        tail = pack[factors:, :].astype(F32)
        lev[:, at] = tail[0:1] + tail[1:2] + tail[2:3]
        label = lax.broadcasted_iota(jnp.int32, (oh.shape[0], points), 0).astype(F32)
        oh[:, at] = (label == tail[3:4]).astype(BF)


def chunk_values(r, w, oh, lev):
    power = jnp.dot(r, w[...], preferred_element_type=F32)
    payoff = jnp.maximum(lev[...] - jnp.exp2(power), 0.0).astype(BF)
    return lax.dot_general(
        payoff, oh[...], (((1,), (1,)), ((), ())), preferred_element_type=F32
    )


def value_kernel(blocks, count, rows, earlier, scale, *refs):
    rts, refs = refs[:blocks], refs[blocks:]
    height = rts[0].shape[1] // 2 + TAIL
    packs = [refs[i].at[r : r + height] for i, r in rows]
    refs = refs[count:]
    before, refs = refs[:earlier], refs[earlier:]
    sources = list(rts)
    if scale:
        basis, refs = refs[: 2 * blocks], refs[2 * blocks :]
        out, w, oh, lev, sems, *held = refs
        sources += basis
    else:
        out, w, oh, lev, sems, *held = refs
    loads = [pltpu.make_async_copy(a, b, sems.at[i]) for i, (a, b) in enumerate(zip(sources, held))]
    for load in loads:
        load.start()
    own = rts[0].shape[0]
    lines = oh.shape[0]
    prepare(packs, w, oh, lev)
    for load in loads[:blocks]:
        load.wait()
    totals = [
        [
            chunk_values(held[i][s0 : s0 + ROWS, :], w, oh, lev)
            for s0 in range(0, own, ROWS)
        ]
        for i in range(blocks)
    ]
    for load in loads[blocks:]:
        load.wait()
    basis = held[blocks:]
    totals = [jnp.concatenate(t, axis=0) for t in totals]
    if not scale:
        out[:, :lines] = totals[0] + before[0][:, :lines]
        out[:, lines:] = totals[1] + before[-1][:, -lines:]
        return
    result = None
    for i in range(blocks):
        v = totals[i] + before[0][:, i * lines : (i + 1) * lines]
        vh = v.astype(BF)
        vl = (v - vh.astype(F32)).astype(BF)
        both = jnp.concatenate([vh, vl], axis=1)
        a = jnp.dot(basis[2 * i][...], both, preferred_element_type=F32)
        b = jnp.dot(basis[2 * i + 1][...], vh, preferred_element_type=F32)
        part = a[:, :lines] + a[:, lines:] + b
        result = part if result is None else result + part
    out[...] = (result * scale).T


def plain_kernel(rt, *refs):
    packs, (out, w, oh, lev, sems, held) = refs[:-6], refs[-6:]
    load = pltpu.make_async_copy(rt, held, sems.at[0])
    load.start()
    prepare(packs, w, oh, lev)
    load.wait()
    rows = TILE // w.shape[1]
    for s0 in range(0, rt.shape[0], rows):
        out[s0 : s0 + rows, :] = chunk_values(held[s0 : s0 + rows, :], w, oh, lev)


VSPEC = pl.BlockSpec(memory_space=pltpu.VMEM)
SSPEC = pl.BlockSpec(memory_space=pltpu.SMEM)
HSPEC = pl.BlockSpec(memory_space=pltpu.HBM)


def like(arrays):
    return [pltpu.VMEM(a.shape, a.dtype) for a in arrays]


def point_scratch(double, lines, points):
    return [
        pltpu.VMEM((double, points), BF),
        pltpu.VMEM((lines, points), BF),
        pltpu.VMEM((1, points), F32),
    ]


def values_of(rts, packs, lines, before=(), basis=(), scale=None, rows=None):
    own, double = rts[0].shape
    points = packs[0].shape[1]
    rows = rows or [(i, 0) for i in range(len(packs))]
    pairs = own * points * len(rts) * len(rows)
    held = [*rts, *basis]
    scratch = point_scratch(double, lines, points * len(rows))
    scratch.append(pltpu.SemaphoreType.DMA((len(held),)))
    kernel = functools.partial(value_kernel, len(rts), len(packs), rows, len(before), scale)
    if scale:
        shape = jax.ShapeDtypeStruct((lines, basis[0].shape[0]), F32)
    else:
        shape = jax.ShapeDtypeStruct((own, lines * len(rts)), F32)
    if not before:
        kernel = plain_kernel
    return pl.pallas_call(
        kernel,
        in_specs=[HSPEC] * len(rts)
        + [VSPEC] * (len(packs) + len(before))
        + [HSPEC] * len(basis),
        out_specs=VSPEC,
        out_shape=shape,
        scratch_shapes=scratch + like(held),
        compiler_params=params(),
        cost_estimate=pl.CostEstimate(
            flops=1700 * pairs, bytes_accessed=2**20, transcendentals=pairs
        ),
    )(*rts, *packs, *before, *basis)


def picks_of(exps):
    count = exps.shape[1]
    e = exps[...].astype(F32)
    row = lax.broadcasted_iota(jnp.int32, (count, count), 0)
    col = lax.broadcasted_iota(jnp.int32, (count, count), 1)
    upto = (row <= col).astype(BF)
    cum = jnp.dot(e.astype(BF), upto, preferred_element_type=F32)
    before = cum - e
    picks = [
        jnp.where((cum > t + 0.5) & (before < t + 0.5), 1.0, 0.0).astype(BF) for t in range(3)
    ]
    return [jnp.concatenate([p, p], axis=1) for p in picks]


def basis_kernel(exps, scens, high, low, rt):
    factors = rt.shape[1] // 2
    r = scens[:factors, :].astype(F32).T.astype(BF)
    rt[:, :factors] = r
    rt[:, factors:] = r
    picks = picks_of(exps)
    for c in range(0, scens.shape[1], CHUNK):
        part = scens[factors:, c : c + CHUNK]
        x = [jnp.dot(p, part, preferred_element_type=F32) for p in picks]
        b = x[0] * x[1] * x[2]
        h = b.astype(BF)
        high[:, c : c + CHUNK] = h
        low[:, c : c + CHUNK] = (b - h.astype(F32)).astype(BF)


def first_kernel(exps, scens, p0, p1, *refs):
    outs, (w, oh, lev, sems, packs, *held) = refs[:4], refs[4:]
    loads = [pltpu.make_async_copy(p, packs.at[i], sems.at[4 + i]) for i, p in enumerate((p0, p1))]
    for load in loads:
        load.start()
    stores = [pltpu.make_async_copy(a, b, sems.at[i]) for i, (a, b) in enumerate(zip(held, outs))]
    basis_kernel(exps, scens, *held[:3])
    for store in stores[:3]:
        store.start()
    for load in loads:
        load.wait()
    prepare([packs.at[0], packs.at[1]], w, oh, lev)
    rows = TILE // w.shape[1]
    for s0 in range(0, held[2].shape[0], rows):
        held[3][s0 : s0 + rows, :] = chunk_values(held[2][s0 : s0 + rows, :], w, oh, lev)
    stores[3].start()
    for store in stores:
        store.wait()


def gram_kernel(start, exps, scens, earlier, *refs):
    outs, keep, send, (sems, both, first, *held) = refs[:3], refs[3], refs[4], refs[5:]
    load = pltpu.make_async_copy(earlier, first, sems.at[3])
    load.start()
    stores = [pltpu.make_async_copy(a, b, sems.at[i]) for i, (a, b) in enumerate(zip(held, outs))]
    high = held[0]
    basis_kernel(exps, scens, *held)
    for store in stores:
        store.start()
    load.wait()
    rows = keep.shape[0]
    r0 = pl.multiple_of(start[0] * (2 * rows), 2 * rows)
    total = None
    for b in (first, high):
        part = lax.dot_general(
            b[pl.ds(r0, 2 * rows), :], b[...], (((1,), (1,)), ((), ())), preferred_element_type=F32
        )
        total = part if total is None else total + part
    both[...] = total
    keep[...] = both[pl.ds(pl.multiple_of(start[1] * rows, rows), rows), :]
    send[...] = both[pl.ds(pl.multiple_of((1 - start[1]) * rows, rows), rows), :]
    for store in stores:
        store.wait()


def basis_of(exponents, scens, near=(), lines=0, start=None, first=None):
    terms, count = exponents.shape
    factors, own = scens.shape[0] - 2 * count, scens.shape[1]
    shapes = [jax.ShapeDtypeStruct((terms, own), BF)] * 2
    shapes.append(jax.ShapeDtypeStruct((own, 2 * factors), BF))
    cost = pl.CostEstimate(flops=3 * 10**9, bytes_accessed=3 * 2**20, transcendentals=0)
    if start is None:
        points = near[0].shape[1]
        shapes.append(jax.ShapeDtypeStruct((own, lines), F32))
        return pl.pallas_call(
            first_kernel,
            in_specs=[VSPEC] * 2 + [HSPEC] * 2,
            out_specs=[HSPEC] * 4,
            out_shape=shapes,
            scratch_shapes=point_scratch(2 * factors, lines, 2 * points)
            + [pltpu.SemaphoreType.DMA((6,)), pltpu.VMEM((2, *near[0].shape), BF)]
            + like(shapes),
            compiler_params=params(),
            cost_estimate=cost,
        )(exponents, scens, *near)
    both = pltpu.VMEM((terms // 2, terms), F32)
    scratch = [pltpu.SemaphoreType.DMA((4,)), both, *like([first]), *like(shapes)]
    shapes += [jax.ShapeDtypeStruct((terms // 4, terms), F32)] * 2
    return pl.pallas_call(
        gram_kernel,
        in_specs=[SSPEC, VSPEC, VSPEC, HSPEC],
        out_specs=[HSPEC] * 3 + [VSPEC] * 2,
        out_shape=shapes,
        scratch_shapes=scratch,
        compiler_params=params(),
        cost_estimate=cost,
    )(start, exponents, scens, first)


def place_kernel(blocks, *refs):
    order, pieces, out = refs[0], refs[1:-1], refs[-1]
    rows = out.shape[0] // blocks
    k = 0
    for piece in pieces:
        for i in range(piece.shape[0] // rows):
            at = pl.multiple_of(order[k] * rows, rows)
            out[pl.ds(at, rows), :] = piece[i * rows : (i + 1) * rows, :]
            k += 1


def placed(blocks, order, pieces, terms):
    return pl.pallas_call(
        functools.partial(place_kernel, blocks),
        in_specs=[pl.BlockSpec(memory_space=pltpu.SMEM)]
        + [pl.BlockSpec(memory_space=pltpu.VMEM)] * len(pieces),
        out_shape=jax.ShapeDtypeStruct((terms, terms), F32),
        compiler_params=params(),
        cost_estimate=pl.CostEstimate(
            flops=2**20, bytes_accessed=2 * 2**20, transcendentals=0
        ),
    )(order, *pieces)


def after(x, done):
    return lax.optimization_barrier((x, done))[0]


def local(n, returns, exposures, guarantees, guar_type, line_ids, drivers, exponents):
    lines = LINES
    scen_total = returns.shape[1] * n
    all_points = exposures.shape[0] * n
    terms = exponents.shape[0]
    me = lax.axis_index("scen").astype(jnp.int32)
    core, side = me & 1, (me >> 1) & 1

    def swap(x, mask):
        return lax.ppermute(x, "scen", [(i, i ^ mask) for i in range(n)])

    deep = [4 << i for i in range((n // 4).bit_length() - 1)]
    scale = 1.0 / (math.sqrt(all_points / lines) * scen_total)
    pack, scens0 = packs_of(exposures, guarantees, guar_type, line_ids, returns, drivers)

    near = (pack, swap(pack, 1))
    scens1 = swap(scens0, 2)
    packs = {m: swap(pack, m) for m in deep}

    high0, low0, rt0, v = basis_of(exponents, scens0, near, lines)
    before = [v]
    packs[4] = after(packs[4], v)
    relay = swap(packs[4], 1)
    far = range(8, n, 4)
    for m in far:
        if m not in packs:
            top = max(h for h in deep if h <= m)
            packs[m] = swap(packs[m ^ top], top)

    base = side * 2 + core
    start = jnp.stack([side, core])
    high1, low1, rt1, keep, send = basis_of(
        exponents, after(scens1, v), start=start, first=high0
    )
    more = swap(send, 1)
    v = values_of([rt1], near, lines)
    before.append(v)
    keep, more = after((keep, more), v)
    gram = (keep + more) * (1.0 / scen_total)

    pairs = [(m, m + 4) for m in range(8, n, 8)]
    calls = [(4,), *pairs, *[(m ^ 1, k ^ 1) for m, k in pairs[:-1]]]
    calls += [(m ^ 1,) for m in pairs[-1]]
    rts = [rt0, rt1]
    steps, other = list(deep), None
    for i, call in enumerate(calls):
        last = i == len(calls) - 1
        if other is not None and (steps or last):
            gram = mine.astype(F32) + after(other, v).astype(F32)
            other = None
        if i == 1:
            for m in far:
                packs[m ^ 1] = swap(after(packs[m], v), 1)
        if steps:
            mine = gram.astype(HALF)
            other = swap(mine, steps.pop(0))
        call = [packs[m] for m in call] + ([relay] if i == 0 else [])
        call = after(call, gram)
        if not last:
            v = values_of(rts, call, lines, before)
            before = [v]
    basis = (high0, low0, high1, low1)
    rhs = values_of(rts, call, lines, before, basis, scale)

    rhs = rhs + swap(rhs, 1)
    for m in [2] + deep:
        mine = rhs.astype(HALF)
        other = swap(mine, m)
        if m == deep[-1]:
            c = swap(jnp.concatenate([a, b], axis=0), 1)
            order = jnp.stack([base ^ k for k in (0, 2, 1, 3)])
            gram = placed(4, order, [x.astype(F32) for x in (a, b, c)], terms)
            other = after(other, gram)
        rhs = mine.astype(F32) + other.astype(F32)
        if m == 2:
            a = after(gram, rhs).astype(HALF)
            b = swap(a, 2)
    return (gram, rhs.T)


def solution(mesh):
    spots = (
        P(None, ("grp", "scen")),
        P(("grp", "scen"), None),
        P(("grp", "scen")),
        P(("grp", "scen")),
        P(("grp", "scen")),
        P(None, ("grp", "scen")),
        P(),
    )
    return jax.shard_map(
        functools.partial(local, mesh.shape["scen"]),
        mesh=mesh,
        in_specs=spots,
        out_specs=(P("grp", None), P("grp", None)),
        check_vma=False,
    )
```

```python
import functools
import math

import jax
import jax.numpy as jnp
from jax import lax
from jax.experimental import pallas as pl
from jax.experimental.pallas import tpu as pltpu
from jax.sharding import PartitionSpec as P

LINES = 64
TAIL = 16
CHUNK = 512
ROWS = 256
TILE = 2**18
LOG2E = 1.4426950408889634
BF = jnp.bfloat16
F32 = jnp.float32
HALF = jnp.float16
VMEM = 24 * 2**20


def params(limit=VMEM):
    return pltpu.CompilerParams(vmem_limit_bytes=limit)


def parts_of(x, count):
    parts = []
    for _ in range(count):
        parts.append(x.astype(BF).astype(F32))
        x = x - parts[-1]
    return parts


def pack_kernel(*refs):
    points, scens = refs[6:8]
    held, sems = refs[8:14], refs[14]
    loads = [pltpu.make_async_copy(refs[i], held[i], sems.at[i]) for i in range(6)]
    for load in loads:
        load.start()
    for load in loads:
        load.wait()
    exposures, guarantees, kinds, lines, returns, drivers = held
    factors = exposures.shape[0]
    points[:factors, :] = exposures[...]
    level = guarantees[...] * (1.0 + 0.15 * kinds[...].astype(F32))
    rows = [*parts_of(level, 3), lines[...].astype(F32)]
    rows.append(jnp.zeros((TAIL - 4, level.shape[1]), F32))
    points[factors:, :] = jnp.concatenate(rows, axis=0).astype(BF)
    scens[:factors, :] = returns[...]
    scens[factors:, :] = jnp.concatenate(parts_of(drivers[...], 2), axis=0).astype(BF)


def packs_of(exposures, guarantees, kinds, lines, returns, drivers):
    points, factors = exposures.shape
    row = (1, points)
    args = (
        exposures.T,
        guarantees.reshape(row),
        kinds.reshape(row),
        lines.reshape(row),
        returns,
        drivers,
    )
    return pl.pallas_call(
        pack_kernel,
        in_specs=[pl.BlockSpec(memory_space=pltpu.HBM)] * len(args),
        out_shape=[
            jax.ShapeDtypeStruct((factors + TAIL, points), BF),
            jax.ShapeDtypeStruct((factors + 2 * drivers.shape[0], returns.shape[1]), BF),
        ],
        scratch_shapes=[pltpu.VMEM(a.shape, a.dtype) for a in args]
        + [pltpu.SemaphoreType.DMA((len(args),))],
        compiler_params=params(58 * 2**20),
        cost_estimate=pl.CostEstimate(flops=2**20, bytes_accessed=2**20, transcendentals=0),
    )(*args)


def prepare(packs, w, oh, lev):
    factors = w.shape[0] // 2
    points = packs[0].shape[1]
    for i, pack in enumerate(packs):
        at = slice(i * points, (i + 1) * points)
        e = pack[:factors, :].astype(F32) * LOG2E
        high = e.astype(BF)
        w[:factors, at] = high
        w[factors:, at] = (e - high.astype(F32)).astype(BF)
        tail = pack[factors:, :].astype(F32)
        lev[:, at] = tail[0:1] + tail[1:2] + tail[2:3]
        label = lax.broadcasted_iota(jnp.int32, (oh.shape[0], points), 0).astype(F32)
        oh[:, at] = (label == tail[3:4]).astype(BF)


def chunk_values(r, w, oh, lev):
    power = jnp.dot(r, w[...], preferred_element_type=F32)
    payoff = jnp.maximum(lev[...] - jnp.exp2(power), 0.0).astype(BF)
    return lax.dot_general(
        payoff, oh[...], (((1,), (1,)), ((), ())), preferred_element_type=F32
    )


def value_kernel(blocks, count, rows, earlier, scale, *refs):
    rts, refs = refs[:blocks], refs[blocks:]
    height = rts[0].shape[1] // 2 + TAIL
    packs = [refs[i].at[r : r + height] for i, r in rows]
    refs = refs[count:]
    before, refs = refs[:earlier], refs[earlier:]
    sources = list(rts)
    if scale:
        basis, refs = refs[: 2 * blocks], refs[2 * blocks :]
        out, w, oh, lev, sems, *held = refs
        sources += basis
    else:
        out, w, oh, lev, sems, *held = refs
    loads = [pltpu.make_async_copy(a, b, sems.at[i]) for i, (a, b) in enumerate(zip(sources, held))]
    for load in loads:
        load.start()
    own = rts[0].shape[0]
    lines = oh.shape[0]
    prepare(packs, w, oh, lev)
    for load in loads[:blocks]:
        load.wait()
    totals = [
        [
            chunk_values(held[i][s0 : s0 + ROWS, :], w, oh, lev)
            for s0 in range(0, own, ROWS)
        ]
        for i in range(blocks)
    ]
    for load in loads[blocks:]:
        load.wait()
    basis = held[blocks:]
    totals = [jnp.concatenate(t, axis=0) for t in totals]
    if not scale:
        out[:, :lines] = totals[0] + before[0][:, :lines]
        out[:, lines:] = totals[1] + before[-1][:, -lines:]
        return
    result = None
    for i in range(blocks):
        v = totals[i] + before[0][:, i * lines : (i + 1) * lines]
        vh = v.astype(BF)
        vl = (v - vh.astype(F32)).astype(BF)
        both = jnp.concatenate([vh, vl], axis=1)
        a = jnp.dot(basis[2 * i][...], both, preferred_element_type=F32)
        b = jnp.dot(basis[2 * i + 1][...], vh, preferred_element_type=F32)
        part = a[:, :lines] + a[:, lines:] + b
        result = part if result is None else result + part
    out[...] = (result * scale).T


def plain_kernel(rt, *refs):
    packs, (out, w, oh, lev) = refs[:-4], refs[-4:]
    prepare(packs, w, oh, lev)
    rows = TILE // w.shape[1]
    for s0 in range(0, rt.shape[0], rows):
        out[s0 : s0 + rows, :] = chunk_values(rt[s0 : s0 + rows, :], w, oh, lev)


VSPEC = pl.BlockSpec(memory_space=pltpu.VMEM)
SSPEC = pl.BlockSpec(memory_space=pltpu.SMEM)
HSPEC = pl.BlockSpec(memory_space=pltpu.HBM)


def like(arrays):
    return [pltpu.VMEM(a.shape, a.dtype) for a in arrays]


def point_scratch(double, lines, points):
    return [
        pltpu.VMEM((double, points), BF),
        pltpu.VMEM((lines, points), BF),
        pltpu.VMEM((1, points), F32),
    ]


def values_of(rts, packs, lines, before=(), basis=(), scale=None, rows=None):
    own, double = rts[0].shape
    points = packs[0].shape[1]
    rows = rows or [(i, 0) for i in range(len(packs))]
    pairs = own * points * len(rts) * len(rows)
    held = [*rts, *basis]
    scratch = point_scratch(double, lines, points * len(rows))
    scratch.append(pltpu.SemaphoreType.DMA((len(held),)))
    kernel = functools.partial(value_kernel, len(rts), len(packs), rows, len(before), scale)
    if scale:
        shape = jax.ShapeDtypeStruct((lines, basis[0].shape[0]), F32)
    else:
        shape = jax.ShapeDtypeStruct((own, lines * len(rts)), F32)
    if not before:
        kernel = plain_kernel
        scratch, held = scratch[:3], []
    return pl.pallas_call(
        kernel,
        in_specs=[HSPEC if before else VSPEC] * len(rts)
        + [VSPEC] * (len(packs) + len(before))
        + [HSPEC] * len(basis),
        out_specs=VSPEC,
        out_shape=shape,
        scratch_shapes=scratch + like(held),
        compiler_params=params(),
        cost_estimate=pl.CostEstimate(
            flops=1700 * pairs, bytes_accessed=2**20, transcendentals=pairs
        ),
    )(*rts, *packs, *before, *basis)


def picks_of(exps):
    count = exps.shape[1]
    e = exps[...].astype(F32)
    row = lax.broadcasted_iota(jnp.int32, (count, count), 0)
    col = lax.broadcasted_iota(jnp.int32, (count, count), 1)
    upto = (row <= col).astype(BF)
    cum = jnp.dot(e.astype(BF), upto, preferred_element_type=F32)
    before = cum - e
    picks = [
        jnp.where((cum > t + 0.5) & (before < t + 0.5), 1.0, 0.0).astype(BF) for t in range(3)
    ]
    return [jnp.concatenate([p, p], axis=1) for p in picks]


def basis_kernel(exps, scens, high, low, rt):
    factors = rt.shape[1] // 2
    r = scens[:factors, :].astype(F32).T.astype(BF)
    rt[:, :factors] = r
    rt[:, factors:] = r
    picks = picks_of(exps)
    for c in range(0, scens.shape[1], CHUNK):
        part = scens[factors:, c : c + CHUNK]
        x = [jnp.dot(p, part, preferred_element_type=F32) for p in picks]
        b = x[0] * x[1] * x[2]
        h = b.astype(BF)
        high[:, c : c + CHUNK] = h
        low[:, c : c + CHUNK] = (b - h.astype(F32)).astype(BF)


def first_kernel(exps, scens, p0, p1, *refs):
    outs, (w, oh, lev, sems, *held) = refs[:4], refs[4:]
    stores = [pltpu.make_async_copy(a, b, sems.at[i]) for i, (a, b) in enumerate(zip(held, outs))]
    basis_kernel(exps, scens, *held[:3])
    for store in stores[:3]:
        store.start()
    prepare([p0, p1], w, oh, lev)
    rows = TILE // w.shape[1]
    for s0 in range(0, held[2].shape[0], rows):
        held[3][s0 : s0 + rows, :] = chunk_values(held[2][s0 : s0 + rows, :], w, oh, lev)
    stores[3].start()
    for store in stores:
        store.wait()


def gram_kernel(start, exps, scens, earlier, *refs):
    outs, keep, send, (sems, both, first, *held) = refs[:3], refs[3], refs[4], refs[5:]
    load = pltpu.make_async_copy(earlier, first, sems.at[3])
    load.start()
    stores = [pltpu.make_async_copy(a, b, sems.at[i]) for i, (a, b) in enumerate(zip(held, outs))]
    high = held[0]
    basis_kernel(exps, scens, *held)
    for store in stores:
        store.start()
    load.wait()
    rows = keep.shape[0]
    r0 = pl.multiple_of(start[0] * (2 * rows), 2 * rows)
    total = None
    for b in (first, high):
        part = lax.dot_general(
            b[pl.ds(r0, 2 * rows), :], b[...], (((1,), (1,)), ((), ())), preferred_element_type=F32
        )
        total = part if total is None else total + part
    both[...] = total
    keep[...] = both[pl.ds(pl.multiple_of(start[1] * rows, rows), rows), :]
    send[...] = both[pl.ds(pl.multiple_of((1 - start[1]) * rows, rows), rows), :]
    for store in stores:
        store.wait()


def basis_of(exponents, scens, near=(), lines=0, start=None, first=None):
    terms, count = exponents.shape
    factors, own = scens.shape[0] - 2 * count, scens.shape[1]
    shapes = [jax.ShapeDtypeStruct((terms, own), BF)] * 2
    shapes.append(jax.ShapeDtypeStruct((own, 2 * factors), BF))
    cost = pl.CostEstimate(flops=3 * 10**9, bytes_accessed=3 * 2**20, transcendentals=0)
    if start is None:
        points = near[0].shape[1]
        shapes.append(jax.ShapeDtypeStruct((own, lines), F32))
        return pl.pallas_call(
            first_kernel,
            in_specs=[VSPEC] * 4,
            out_specs=[HSPEC] * 4,
            out_shape=shapes,
            scratch_shapes=point_scratch(2 * factors, lines, 2 * points)
            + [pltpu.SemaphoreType.DMA((4,))]
            + like(shapes),
            compiler_params=params(),
            cost_estimate=cost,
        )(exponents, scens, *near)
    both = pltpu.VMEM((terms // 2, terms), F32)
    scratch = [pltpu.SemaphoreType.DMA((4,)), both, *like([first]), *like(shapes)]
    shapes += [jax.ShapeDtypeStruct((terms // 4, terms), F32)] * 2
    return pl.pallas_call(
        gram_kernel,
        in_specs=[SSPEC, VSPEC, VSPEC, HSPEC],
        out_specs=[HSPEC] * 3 + [VSPEC] * 2,
        out_shape=shapes,
        scratch_shapes=scratch,
        compiler_params=params(),
        cost_estimate=cost,
    )(start, exponents, scens, first)


def place_kernel(blocks, *refs):
    order, pieces, out = refs[0], refs[1:-1], refs[-1]
    rows = out.shape[0] // blocks
    k = 0
    for piece in pieces:
        for i in range(piece.shape[0] // rows):
            at = pl.multiple_of(order[k] * rows, rows)
            out[pl.ds(at, rows), :] = piece[i * rows : (i + 1) * rows, :]
            k += 1


def placed(blocks, order, pieces, terms):
    return pl.pallas_call(
        functools.partial(place_kernel, blocks),
        in_specs=[pl.BlockSpec(memory_space=pltpu.SMEM)]
        + [pl.BlockSpec(memory_space=pltpu.VMEM)] * len(pieces),
        out_shape=jax.ShapeDtypeStruct((terms, terms), F32),
        compiler_params=params(),
        cost_estimate=pl.CostEstimate(
            flops=2**20, bytes_accessed=2 * 2**20, transcendentals=0
        ),
    )(order, *pieces)


def after(x, done):
    return lax.optimization_barrier((x, done))[0]


def local(n, returns, exposures, guarantees, guar_type, line_ids, drivers, exponents):
    lines = LINES
    scen_total = returns.shape[1] * n
    all_points = exposures.shape[0] * n
    terms = exponents.shape[0]
    me = lax.axis_index("scen").astype(jnp.int32)
    core, side = me & 1, (me >> 1) & 1

    def swap(x, mask):
        return lax.ppermute(x, "scen", [(i, i ^ mask) for i in range(n)])

    deep = [4 << i for i in range((n // 4).bit_length() - 1)]
    scale = 1.0 / (math.sqrt(all_points / lines) * scen_total)
    pack, scens0 = packs_of(exposures, guarantees, guar_type, line_ids, returns, drivers)

    near = (pack, swap(pack, 1))
    scens1 = swap(scens0, 2)
    packs = {m: swap(pack, m) for m in deep}

    high0, low0, rt0, v = basis_of(exponents, scens0, near, lines)
    before = [v]
    packs[4] = after(packs[4], v)
    relay = swap(packs[4], 1)
    far = range(8, n, 4)
    for m in far:
        if m not in packs:
            top = max(h for h in deep if h <= m)
            packs[m] = swap(packs[m ^ top], top)

    base = side * 2 + core
    start = jnp.stack([side, core])
    high1, low1, rt1, keep, send = basis_of(
        exponents, after(scens1, v), start=start, first=high0
    )
    more = swap(send, 1)
    v = values_of([rt1], near, lines)
    before.append(v)
    keep, more = after((keep, more), v)
    gram = (keep + more) * (1.0 / scen_total)

    pairs = [(m, m + 4) for m in range(8, n, 8)]
    calls = [(4,), *pairs, *[(m ^ 1, k ^ 1) for m, k in pairs[:-1]]]
    calls += [(m ^ 1,) for m in pairs[-1]]
    rts = [rt0, rt1]
    steps, other = list(deep), None
    for i, call in enumerate(calls):
        last = i == len(calls) - 1
        if other is not None and (steps or last):
            gram = mine.astype(F32) + after(other, v).astype(F32)
            other = None
        if i == 1:
            for m in far:
                packs[m ^ 1] = swap(after(packs[m], v), 1)
        if steps:
            mine = gram.astype(HALF)
            other = swap(mine, steps.pop(0))
        call = [packs[m] for m in call] + ([relay] if i == 0 else [])
        call = after(call, gram)
        if not last:
            v = values_of(rts, call, lines, before)
            before = [v]
    basis = (high0, low0, high1, low1)
    rhs = values_of(rts, call, lines, before, basis, scale)

    rhs = rhs + swap(rhs, 1)
    for m in [2] + deep:
        mine = rhs.astype(HALF)
        other = swap(mine, m)
        if m == deep[-1]:
            c = swap(jnp.concatenate([a, b], axis=0), 1)
            order = jnp.stack([base ^ k for k in (0, 2, 1, 3)])
            gram = placed(4, order, [x.astype(F32) for x in (a, b, c)], terms)
            other = after(other, gram)
        rhs = mine.astype(F32) + other.astype(F32)
        if m == 2:
            a = after(gram, rhs).astype(HALF)
            b = swap(a, 2)
    return (gram, rhs.T)


def solution(mesh):
    spots = (
        P(None, ("grp", "scen")),
        P(("grp", "scen"), None),
        P(("grp", "scen")),
        P(("grp", "scen")),
        P(("grp", "scen")),
        P(None, ("grp", "scen")),
        P(),
    )
    return jax.shard_map(
        functools.partial(local, mesh.shape["scen"]),
        mesh=mesh,
        in_specs=spots,
        out_specs=(P("grp", None), P("grp", None)),
        check_vma=False,
    )
```
